32 devices in a mesh: tm: 4 (over y, x), space: 2 (over core), head: 4 (over z).
Axes of the slice: x: 2, y: 2, z: 4, core: 2. Of those that a mesh axis runs over, the one named last changes fastest.
Arguments:
- query: bfloat16 [4, 8, 80, 5120], P('tm', 'space', None, 'head'), may hold values from -5 to 5
- key: bfloat16 [4, 8, 80, 5120], P('tm', 'space', None, 'head'), may hold values from -5 to 5
- value: bfloat16 [4, 8, 80, 5120], P('tm', 'space', None, 'head'), may hold values from -6 to 6
- window: int32 [4, 4], replicated, may hold values from -1 to 4, as said below
- out_weight: bfloat16 [5120, 5120], P('head'), may hold values from -0.078125 to 0.078125
Outputs:
- projected: bfloat16 [4, 8, 80, 5120], P('tm', 'space', None, 'head')
The draws below stay inside these ranges and needn't reach their ends.
Inputs may be any that keep to these rules, and one draw needn't show every extreme that they name: window[f, f] = 4 for every frame f.
All inputs are finite; a program needn't handle non-finite values.
Results may differ from the reference program's by a relative error of at most 0.023.
Values may be sent and summed in bfloat16 or wider, within the bound.
No kernel may reach another device: no remote copies, remote signals or barrier semaphores. Data moves between devices by JAX's collectives and lax.ppermute only.
A program may use at most 128 MiB of HBM per device.

```python
import math
import jax
import jax.numpy as jnp
from jax import lax

HD = 128
D = 5120
WIDTH = 80
HALO = 4
FRAMES = 4
ROWS = 8


def drawn_pair(key):
    base_stream = jax.random.fold_in(key, 11)
    query_stream, key_stream = jax.random.split(base_stream, 2)
    shape = (FRAMES, ROWS, WIDTH, D)
    query_part = jnp.clip(jax.random.normal(query_stream, shape, jnp.float32), -5.0, 5.0)
    key_part = jnp.clip(jax.random.normal(key_stream, shape, jnp.float32), -5.0, 5.0)
    return (query_part, key_part)


def draw_query(key, part):
    return drawn_pair(key)[0].astype(jnp.bfloat16)


def draw_key(key, part):
    return drawn_pair(key)[1].astype(jnp.bfloat16)


def draw_window(key, part):
    stream = jax.random.fold_in(key, 23)
    raw_width = jax.random.randint(stream, (FRAMES, FRAMES), -1, HALO + 1)
    first = jnp.arange(FRAMES, dtype=jnp.int32)[:, None]
    second = jnp.arange(FRAMES, dtype=jnp.int32)[None, :]
    distance = jnp.abs(first - second)
    ceiling = HALO - (HALO + 1) * distance // FRAMES
    banded = jnp.maximum(jnp.minimum(raw_width, ceiling), -1)
    return jnp.where(distance == 0, HALO, banded).astype(jnp.int32)


def block_levels(rng, shape, shards, smallest, largest):
    level = 1.0
    for position, blocks in shards:
        draws = jax.random.uniform(jax.random.fold_in(jax.random.fold_in(rng, 6), position), (blocks,), jnp.float32, smallest / len(shards), largest / len(shards))
        level = level * jnp.repeat(jnp.exp(draws), shape[position] // blocks).reshape((-1,) + (1,) * (len(shape) - 1 - position))
    return level


def bell_draw(stream_key, dims, scale, limit, shards=(), held_as=jnp.bfloat16):
    drawn = scale * jax.random.normal(stream_key, dims, jnp.float32)
    if shards:
        drawn = drawn * block_levels(stream_key, dims, shards, -0.22, 0.18)
    return jnp.clip(drawn, -limit, limit).astype(held_as)


def setup_inputs(seed: int = 0) -> dict:
    keys = jax.random.split(jax.random.key(seed), 6)
    return {
        "query": draw_query(jax.random.fold_in(keys[5], 71), 0),
        "key": draw_key(jax.random.fold_in(keys[5], 71), 0),
        "value": bell_draw(keys[2], (FRAMES, ROWS, WIDTH, D), 1.0, 6.0, ((0, 4), (1, 2), (3, 4))),
        "window": draw_window(jax.random.fold_in(keys[5], 71), 0),
        "out_weight": bell_draw(keys[4], (D, D), D ** -0.5, 0.078125, ((0, 4),)),
    }


NEG_FILL = -1e+30

def reference(query, key, value, window, out_weight):
    frames, rows, width, feats = query.shape
    heads = feats // HD
    tokens = frames * rows * width
    per_frame = rows * width
    all_keys = key.reshape(tokens, heads, HD).transpose(1, 0, 2)
    all_values = value.reshape(tokens, heads, HD).transpose(1, 0, 2)
    all_queries = query.reshape(frames, per_frame, heads, HD).transpose(0, 2, 1, 3)
    row_ids = jnp.arange(rows, dtype=jnp.int32)
    distance = jnp.abs(row_ids[:, None] - row_ids[None, :])
    scale = 1.0 / math.sqrt(HD)

    def attend(index):
        frame = index // heads
        head = index % heads
        frame_query = lax.dynamic_index_in_dim(lax.dynamic_index_in_dim(all_queries, frame, 0, False), head, 0, False)
        head_keys = lax.dynamic_index_in_dim(all_keys, head, 0, False)
        head_values = lax.dynamic_index_in_dim(all_values, head, 0, False)
        widths = lax.dynamic_index_in_dim(window, frame, 0, False)
        inside = (widths[None, :, None] >= 0) & (distance[:, None, :] <= widths[None, :, None])
        mask = jnp.broadcast_to(inside[:, None, :, :, None], (rows, width, frames, rows, width)).reshape(per_frame, tokens)
        scores = jnp.dot(frame_query, head_keys.T, preferred_element_type=jnp.float32) * scale
        top = lax.optimization_barrier(jnp.max(jnp.where(mask, scores, NEG_FILL), axis=-1))
        weights = jnp.where(mask, jnp.exp(scores - top[:, None]), 0.0)
        summed = jnp.dot(weights.astype(jnp.bfloat16), head_values, preferred_element_type=jnp.float32)
        return summed / lax.optimization_barrier(jnp.sum(weights, axis=-1))[:, None]
    outputs = lax.map(attend, jnp.arange(frames * heads, dtype=jnp.int32))
    attended = outputs.reshape(frames, heads, per_frame, HD).transpose(0, 2, 1, 3).reshape(tokens, feats).astype(jnp.bfloat16)
    projected = jnp.dot(attended, out_weight, preferred_element_type=jnp.float32).astype(jnp.bfloat16)
    return projected.reshape(frames, rows, width, feats)
```

```python
import math

import jax
import jax.numpy as jnp
from jax import lax
from jax.experimental import pallas as pl
from jax.experimental.pallas import tpu as pltpu
from jax.sharding import PartitionSpec as P

HD = 128
HALO = 4
NEG_FILL = -1e30
CHUNKS = 2
VMEM = pltpu.CompilerParams(vmem_limit_bytes=40 * 1024 * 1024)


def pack_kernel(t_ref, q_ref, k_ref, v_ref, *outs, full, share, row):
    t = t_ref[0]
    tokens = q_ref.shape[0]
    partners = len(outs) // (1 + CHUNKS)
    part = tokens // CHUNKS
    for m in range(partners):
        chip = t ^ m
        heads = [chip * full + i for i in range(full)] + [partners * full + chip // share]
        lanes = [pl.ds(pl.multiple_of(h * HD, HD), HD) for h in heads]
        kv = outs[m]
        for i, lane in enumerate(lanes):
            kv[pl.ds(i * tokens, tokens)] = k_ref[:, lane]
            kv[pl.ds((full + 1 + i) * tokens, tokens)] = v_ref[:, lane]
        for c in range(CHUNKS):
            q = outs[(1 + c) * partners + m]
            for i in range(full):
                q[pl.ds(i * part, part)] = q_ref[pl.ds(c * part, part), lanes[i]]
            start = pl.multiple_of(c * part + (chip % share) * row, 16)
            q[pl.ds(full * part, row)] = q_ref[pl.ds(start, row), lanes[full]]


def pack(t, q, k, v, partners, full, share, row):
    tokens = q.shape[0]
    part = tokens // CHUNKS
    slabs = 2 * (full + 1) * tokens
    queries = full * part + row
    whole = pl.BlockSpec(memory_space=pltpu.VMEM)
    shapes = [jax.ShapeDtypeStruct((slabs, HD), q.dtype)] * partners
    shapes += [jax.ShapeDtypeStruct((queries, HD), q.dtype)] * (partners * CHUNKS)

    def kernel(*refs):
        pack_kernel(*refs, full=full, share=share, row=row)

    return pl.pallas_call(
        kernel,
        out_shape=shapes,
        in_specs=[pl.BlockSpec(memory_space=pltpu.SMEM), whole, whole, whole],
        out_specs=[whole] * len(shapes),
        compiler_params=VMEM,
        name="pack",
    )(t, q, k, v)


def attend_kernel(bias_ref, *refs, partners, slots, row, units):
    queries = refs[:partners]
    near = refs[partners : 2 * partners]
    far = refs[2 * partners : 3 * partners]
    outs = refs[3 * partners : 4 * partners]
    keys, values, scores, sems = refs[4 * partners :]
    tokens = near[0].shape[0] // (2 * slots)
    count = keys.shape[1]
    copies = []
    for slot in range(slots):
        for m in range(partners):
            for side, source in enumerate((near[m], far[m])):
                place = pl.ds((2 * m + side) * tokens, tokens)
                for kind, target in enumerate((keys.at[slot, place], values.at[slot, place, pl.ds(0, HD)])):
                    start = (kind * slots + slot) * tokens
                    copy = pltpu.make_async_copy(
                        source.at[pl.ds(start, tokens)], target, sems.at[len(copies)]
                    )
                    copy.start()
                    copies.append(copy)
    values[:, :, HD:] = jnp.ones((slots, count, HD), values.dtype)
    for copy in copies:
        copy.wait()
    factor = math.log2(math.e) / math.sqrt(HD)
    per_slot = units // (slots - 1) if units > 1 else 1

    def unit(u, carry):
        slot = u // per_slot
        at = pl.ds(pl.multiple_of(u * row, 16), row)
        for m in range(partners):
            s = lax.dot_general(
                queries[m][at], keys[slot], (((1,), (1,)), ((), ())), preferred_element_type=jnp.float32
            )
            s = s + bias_ref[u * partners + m]
            top = jnp.max(s, axis=-1, keepdims=True)
            weights = jnp.exp2((s - top) * factor).astype(jnp.bfloat16)
            summed = jnp.dot(weights, values[slot], preferred_element_type=jnp.float32)
            outs[m][at] = (summed[:, :HD] / summed[:, HD:]).astype(jnp.bfloat16)
        return carry

    lax.fori_loop(0, units, unit, 0)


def attend(bias, queries, near, far, slots, row):
    partners = len(queries)
    units = queries[0].shape[0] // row
    tokens = near[0].shape[0] // (2 * slots)
    count = 2 * partners * tokens
    whole = pl.BlockSpec(memory_space=pltpu.VMEM)
    anywhere = pl.BlockSpec(memory_space=pl.ANY)

    def kernel(*refs):
        attend_kernel(*refs, partners=partners, slots=slots, row=row, units=units)

    work = units * partners * row * count
    return pl.pallas_call(
        kernel,
        out_shape=[jax.ShapeDtypeStruct(q.shape, q.dtype) for q in queries],
        in_specs=[whole] * (1 + partners) + [anywhere] * (2 * partners),
        out_specs=[whole] * partners,
        scratch_shapes=[
            pltpu.VMEM((slots, count, HD), jnp.bfloat16),
            pltpu.VMEM((slots, count, 2 * HD), jnp.bfloat16),
            pltpu.VMEM((row, count), jnp.float32),
            pltpu.SemaphoreType.DMA((4 * slots * partners,)),
        ],
        compiler_params=VMEM,
        cost_estimate=pl.CostEstimate(
            flops=work * HD * 4, bytes_accessed=count * HD * 4 * slots, transcendentals=work
        ),
        name="attend",
    )(bias, *queries, *near, *far)


def project_kernel(t_ref, *refs, partners, full, share, row):
    parts = refs[:partners]
    weight, out, mixed = refs[partners:]
    part = mixed.shape[0]

    @pl.when(pl.program_id(0) == 0)
    def gather():
        for m in range(partners):
            chip = t_ref[0] ^ m
            for i in range(full):
                lane = pl.ds(pl.multiple_of((chip * full + i) * HD, HD), HD)
                mixed[:, lane] = parts[m][pl.ds(i * part, part)]
            lane = pl.ds(pl.multiple_of((partners * full + chip // share) * HD, HD), HD)
            rows = pl.ds(pl.multiple_of((chip % share) * row, 16), row)
            mixed[rows, lane] = parts[m][pl.ds(full * part, row)]

    out[0] = jnp.dot(mixed[...], weight[...], preferred_element_type=jnp.float32).astype(out.dtype)


def project(t, parts, weight, shares, full, share, row):
    partners = len(parts)
    feats, width = weight.shape
    part = (parts[0].shape[0] - row) // full
    block = width // shares
    whole = pl.BlockSpec(memory_space=pltpu.VMEM)

    def kernel(*refs):
        project_kernel(*refs, partners=partners, full=full, share=share, row=row)

    return pl.pallas_call(
        kernel,
        grid=(shares,),
        out_shape=jax.ShapeDtypeStruct((shares, part, block), jnp.bfloat16),
        in_specs=[pl.BlockSpec(memory_space=pltpu.SMEM)]
        + [whole] * partners
        + [pl.BlockSpec((feats, block), lambda i: (0, i))],
        out_specs=pl.BlockSpec((1, part, block), lambda i: (i, 0, 0)),
        scratch_shapes=[pltpu.VMEM((part, feats), jnp.bfloat16)],
        compiler_params=VMEM,
        cost_estimate=pl.CostEstimate(
            flops=2 * part * feats * width, bytes_accessed=2 * feats * width, transcendentals=0
        ),
        name="project",
    )(t, *parts, weight)


def scatter_sum(mixed, axis):
    size = lax.axis_size(axis)
    place = lax.axis_index(axis)

    def share(d):
        return lax.dynamic_index_in_dim(mixed, jnp.clip(d, 0, size - 1), 0, False)

    right = left = None
    for step in range(1, size):
        go_right = share(place + size - step)
        go_left = share(place - size + step)
        if right is not None:
            go_right, go_left = go_right + right, go_left + left
        right = lax.ppermute(go_right, axis, [(i, i + 1) for i in range(step)])
        left = lax.ppermute(go_left, axis, [(size - 1 - i, size - 2 - i) for i in range(step)])
    return share(place) + right + left


def exchange_plan(query, key, value, window, out_weight):
    frames_dev, rows_dev, width, feats = query.shape
    partners = lax.axis_size("tm")
    heads = feats // HD
    full = heads // partners
    share = partners // (heads - full * partners)
    t = lax.axis_index("tm").astype(jnp.int32)
    s = lax.axis_index("space").astype(jnp.int32)
    tokens = rows_dev * width
    rows_part = rows_dev // CHUNKS
    t1 = t.reshape(1)

    packed = pack(
        t1, *(a.reshape(tokens, feats) for a in (query, key, value)), partners, full, share, width
    )
    near, asked = packed[:partners], packed[partners:]

    def swap(x, m):
        return x if m == 0 else lax.ppermute(x, "tm", [(i, i ^ m) for i in range(partners)])

    near = [swap(x, m) for m, x in enumerate(near)]
    far = [lax.ppermute(x, "space", [(0, 1), (1, 0)]) for x in near]

    order = t ^ jnp.arange(partners, dtype=jnp.int32)
    widths = window[order][:, order]
    units = full * rows_part + 1
    key_rows = jnp.concatenate([rows_dev * side + jnp.arange(rows_dev, dtype=jnp.int32) for side in (s, 1 - s)])
    unit_rows = jnp.concatenate([jnp.arange(units - 1, dtype=jnp.int32) % rows_part, (t % share)[None]])
    query_rows = rows_dev * s + rows_part * jnp.arange(CHUNKS, dtype=jnp.int32)[:, None] + unit_rows[None]
    distance = jnp.abs(query_rows[:, :, None] - key_rows)[:, :, None, None, :]
    wide = widths[None, None, :, :, None]
    bias = jnp.where((wide >= 0) & (distance <= wide), 0.0, NEG_FILL).astype(jnp.float32)
    bias = jnp.repeat(bias, width, axis=-1).reshape(CHUNKS, units * partners, 1, -1)

    outputs = []
    for c in range(CHUNKS):
        queries = [swap(x, m) for m, x in enumerate(asked[c * partners : (c + 1) * partners])]
        done = attend(bias[c], queries, near, far, full + 1, width)
        done = [swap(x, m) for m, x in enumerate(done)]
        mixed = project(t1, done, out_weight, lax.axis_size("head"), full, share, width)
        outputs.append(scatter_sum(mixed, "head"))
    return jnp.concatenate(outputs, axis=0).reshape(frames_dev, rows_dev, width, -1)


def can_exchange(mesh, query, key, value, window, out_weight):
    partners, sides = mesh.shape["tm"], mesh.shape["space"]
    frames, rows, width, feats = query.shape
    heads = feats // HD // mesh.shape["head"]
    rows_dev = rows // sides
    rest = heads % partners
    if partners & (partners - 1) or sides != 2 or frames != partners or rest == 0 or heads < partners:
        return False
    return partners % rest == 0 and rows_dev == CHUNKS * (partners // rest) and width % 16 == 0


def padded_2(x, sides, width):
    for axis, dim in sides:
        size, length = (lax.axis_size(axis), x.shape[dim])
        up = [(i, (i + 1) % size) for i in range(size - 1)]
        down = [(j, i) for i, j in up]
        last = lax.slice_in_dim(x, length - width, length, axis=dim)
        first = lax.slice_in_dim(x, 0, width, axis=dim)
        before = lax.ppermute(last, axis, up)
        after = lax.ppermute(first, axis, down)
        x = jnp.concatenate([before, x, after], axis=dim)
    return x


def frame_mask(widths, query_rows, key_rows, total_rows, width):
    count = widths.shape[0]
    distance = jnp.abs(query_rows[:, None] - key_rows[None, :])
    inside_grid = (key_rows >= 0) & (key_rows < total_rows)
    inside = (
        (widths[:, None, None] >= 0)
        & (distance[None] <= widths[:, None, None])
        & inside_grid[None, None, :]
    )
    span_rows = key_rows.shape[0]
    full = jnp.broadcast_to(
        inside[:, :, None, :, None], (count, query_rows.shape[0], width, span_rows, width)
    )
    return full.reshape(count * query_rows.shape[0] * width, span_rows * width)


def absorb(state, queries, keys, values, mask):
    run_max, run_sum, run_acc = state
    scale = 1.0 / math.sqrt(HD)
    scores = jnp.einsum("qhd,khd->hqk", queries, keys, preferred_element_type=jnp.float32) * scale
    new_max = jnp.maximum(run_max, jnp.max(jnp.where(mask[None], scores, NEG_FILL), axis=-1))
    weights = jnp.where(mask[None], jnp.exp(scores - new_max[..., None]), 0.0)
    factor = jnp.exp(run_max - new_max)
    new_sum = run_sum * factor + jnp.sum(weights, axis=-1)
    new_acc = run_acc * factor[..., None] + jnp.einsum(
        "hqk,khd->hqd", weights.astype(jnp.bfloat16), values, preferred_element_type=jnp.float32
    )
    return (new_max, new_sum, new_acc)


def absorb_frame(state, queries, widths, kv_frame, query_rows, key_rows, total_rows):
    span_rows, width, feats = (kv_frame.shape[1], kv_frame.shape[2], kv_frame.shape[3])
    heads_dev = feats // HD
    keys = kv_frame[0].reshape(span_rows * width, heads_dev, HD)
    values = kv_frame[1].reshape(span_rows * width, heads_dev, HD)
    mask = frame_mask(widths, query_rows, key_rows, total_rows, width)
    return absorb(state, queries, keys, values, mask)


def empty_state(heads_dev, count):
    return (
        jnp.full((heads_dev, count), NEG_FILL, jnp.float32),
        jnp.zeros((heads_dev, count), jnp.float32),
        jnp.zeros((heads_dev, count, HD), jnp.float32),
    )


def gather_plan(query, key, value, window, out_weight):
    frames_dev, rows_dev, width, feats = query.shape
    heads_dev = feats // HD
    qcount = frames_dev * rows_dev * width
    total_rows = rows_dev * lax.axis_size("space")
    first_row = lax.axis_index("space") * rows_dev
    first_frame = lax.axis_index("tm") * frames_dev
    query_rows = first_row + jnp.arange(rows_dev, dtype=jnp.int32)
    stacked = jnp.stack([key, value])
    padded = padded_2(stacked, (("space", 2),), HALO)
    key_rows = first_row - HALO + jnp.arange(rows_dev + 2 * HALO, dtype=jnp.int32)
    my_windows = lax.dynamic_slice_in_dim(window, first_frame, frames_dev, 0)
    queries = query.reshape(qcount, heads_dev, HD)
    piece = lax.all_gather(padded, "tm", axis=1, tiled=True)

    def one_frame(carry, offset):
        kv_frame = lax.dynamic_index_in_dim(piece, offset, 1, False)
        widths = lax.dynamic_index_in_dim(my_windows, offset, 1, False)
        return (
            absorb_frame(carry, queries, widths, kv_frame, query_rows, key_rows, total_rows),
            None,
        )

    result, unused = lax.scan(
        one_frame, empty_state(heads_dev, qcount), jnp.arange(piece.shape[1], dtype=jnp.int32)
    )
    run_max, run_sum, run_acc = result
    attended = (
        (run_acc / run_sum[..., None])
        .transpose(1, 0, 2)
        .reshape(qcount, feats)
        .astype(jnp.bfloat16)
    )
    share_rows = out_weight.shape[1] // lax.axis_size("head")
    mixed = lax.psum_scatter(
        lax.dot_general(
            out_weight, attended, (((0,), (1,)), ((), ())), preferred_element_type=jnp.float32
        ).astype(jnp.bfloat16),
        "head",
        scatter_dimension=0,
        tiled=True,
    ).astype(jnp.float32)
    return mixed.T.reshape(frames_dev, rows_dev, width, share_rows).astype(jnp.bfloat16)


def solution(mesh):
    placed = (
        P("tm", "space", None, "head"),
        P("tm", "space", None, "head"),
        P("tm", "space", None, "head"),
        P(),
        P("head", None),
    )

    def run(*args):
        body = exchange_plan if can_exchange(mesh, *args) else gather_plan
        return jax.shard_map(
            body, mesh=mesh, in_specs=placed, out_specs=P("tm", "space", None, "head"), check_vma=False
        )(*args)

    return run
```

```python
import math

import jax
import jax.numpy as jnp
from jax import lax
from jax.experimental import pallas as pl
from jax.experimental.pallas import tpu as pltpu
from jax.sharding import PartitionSpec as P

HD = 128
HALO = 4
NEG_FILL = -1e30
CHUNKS = 2
VMEM = pltpu.CompilerParams(vmem_limit_bytes=32 * 1024 * 1024)


def pack_kernel(t_ref, q_ref, k_ref, v_ref, first, *rest, partner, partners, full, share, row):
    sems = rest[-1]
    tokens = q_ref.shape[0]
    part = tokens // CHUNKS
    chip = t_ref[0] ^ partner
    heads = [chip * full + i for i in range(full)] + [partners * full + chip // share]
    lanes = [pl.ds(pl.multiple_of(h * HD, HD), HD) for h in heads]
    moves = []
    for kind, source in enumerate((k_ref, v_ref)):
        for i, lane in enumerate(lanes):
            place = pl.ds((kind * (full + 1) + i) * tokens, tokens)
            moves.append((source.at[:, lane], first.at[place]))
    for c in range(CHUNKS):
        target, base = (first, 2 * (full + 1) * tokens) if c == 0 else (rest[c - 1], 0)
        for i in range(full):
            moves.append((q_ref.at[pl.ds(c * part, part), lanes[i]], target.at[pl.ds(base + i * part, part)]))
        start = pl.multiple_of(c * part + (chip % share) * row, 16)
        moves.append((q_ref.at[pl.ds(start, row), lanes[full]], target.at[pl.ds(base + full * part, row)]))
    copies = [pltpu.make_async_copy(a, b, sems.at[n]) for n, (a, b) in enumerate(moves)]
    for copy in copies:
        copy.start()
    for copy in copies:
        copy.wait()


def pack(t, q, k, v, partner, partners, full, share, row):
    tokens = q.shape[0]
    queries = full * (tokens // CHUNKS) + row
    slabs = 2 * (full + 1) * tokens + queries
    whole = pl.BlockSpec(memory_space=pltpu.VMEM)
    anywhere = pl.BlockSpec(memory_space=pl.ANY)
    shapes = [jax.ShapeDtypeStruct((slabs, HD), q.dtype)]
    shapes += [jax.ShapeDtypeStruct((queries, HD), q.dtype)] * (CHUNKS - 1)

    def kernel(*refs):
        pack_kernel(*refs, partner=partner, partners=partners, full=full, share=share, row=row)

    return pl.pallas_call(
        kernel,
        out_shape=shapes,
        in_specs=[pl.BlockSpec(memory_space=pltpu.SMEM), anywhere, anywhere, anywhere],
        out_specs=[whole] * len(shapes),
        scratch_shapes=[pltpu.SemaphoreType.DMA(((full + 1) * (2 + CHUNKS),))],
        compiler_params=VMEM,
        name="pack",
    )(t, q, k, v)


def attend_kernel(
    place_ref, window_ref, *refs, chunk, partners, full, share, row, rows_dev, total_rows, asked
):
    queries = refs[:partners]
    near = refs[partners : 2 * partners]
    far = refs[2 * partners : 3 * partners]
    outs = refs[3 * partners :]
    slots = full + 1
    tokens = rows_dev * row
    count = 2 * partners * tokens
    t, s = place_ref[0], place_ref[1]
    rows_part = rows_dev // CHUNKS
    factor = math.log2(math.e) / math.sqrt(HD)

    at = lax.broadcasted_iota(jnp.int32, (1, count), 1)
    frame = at // (2 * tokens)
    side = (at // tokens) % 2
    key_row = (at % tokens) // row + rows_dev * jnp.where(side == 0, s, 1 - s)
    widths = []
    for m in range(partners):
        wide = jnp.zeros_like(at)
        for m2 in range(partners):
            wide = jnp.where(frame == m2, window_ref[t ^ m, t ^ m2], wide)
        widths.append(wide)

    def bias(unit, m):
        part_row = unit % rows_part if unit < full * rows_part else t % share
        distance = jnp.abs(key_row - (rows_dev * s + rows_part * chunk + part_row))
        return jnp.where(distance <= widths[m], 0.0, NEG_FILL).astype(jnp.float32)

    def block(kind, slot):
        base = (kind * slots + slot) * tokens
        return jnp.concatenate([r[pl.ds(base, tokens)] for m in range(partners) for r in (near[m], far[m])], axis=0)

    def score(tile):
        unit, pair = tile
        q = jnp.concatenate([queries[m][pl.ds(asked + unit * row, row)] for m in pair], axis=0)
        return lax.dot_general(
            q, block(0, unit // rows_part), (((1,), (1,)), ((), ())), preferred_element_type=jnp.float32
        )

    def weigh(tile, scores):
        unit, pair = tile
        scores = jnp.concatenate(
            [scores[i * row : (i + 1) * row] + bias(unit, m) for i, m in enumerate(pair)], axis=0
        )
        top = jnp.max(scores, axis=-1, keepdims=True)
        return jnp.exp2((scores - top) * factor).astype(jnp.bfloat16)

    def gather(tile, weights):
        unit, pair = tile
        held = block(1, unit // rows_part)
        held = jnp.concatenate([held, jnp.ones_like(held)], axis=1)
        summed = jnp.dot(weights, held, preferred_element_type=jnp.float32)
        out = (summed[:, :HD] / summed[:, HD:]).astype(jnp.bfloat16)
        for i, m in enumerate(pair):
            outs[m][pl.ds(unit * row, row)] = out[i * row : (i + 1) * row]

    pairs = [tuple(range(m, m + 2)) for m in range(0, partners, 2)]
    tiles = [(unit, pair) for unit in range(full * rows_part + 1) for pair in pairs]
    scores, last = score(tiles[0]), None
    for i, tile in enumerate(tiles):
        following = score(tiles[i + 1]) if i + 1 < len(tiles) else None
        if last is not None:
            gather(*last)
        last = (tile, weigh(tile, scores))
        scores = following
    gather(*last)


def attend(place, window, queries, near, far, chunk, full, share, row, rows_dev):
    partners = len(queries)
    rows_out = full * (rows_dev // CHUNKS) * row + row
    count = 2 * partners * rows_dev * row
    whole = pl.BlockSpec(memory_space=pltpu.VMEM)
    scalars = pl.BlockSpec(memory_space=pltpu.SMEM)

    def kernel(*refs):
        attend_kernel(
            *refs,
            chunk=chunk,
            partners=partners,
            full=full,
            share=share,
            row=row,
            rows_dev=rows_dev,
            total_rows=2 * rows_dev,
            asked=queries[0].shape[0] - rows_out,
        )

    work = partners * rows_out * count
    return pl.pallas_call(
        kernel,
        out_shape=[jax.ShapeDtypeStruct((rows_out, HD), jnp.bfloat16)] * partners,
        in_specs=[scalars, scalars] + [whole] * (3 * partners),
        out_specs=[whole] * partners,
        compiler_params=VMEM,
        cost_estimate=pl.CostEstimate(
            flops=work * HD * 4, bytes_accessed=count * HD * 4 * (full + 1), transcendentals=work
        ),
        name="attend",
    )(place, window, *queries, *near, *far)


def project_kernel(t_ref, *refs, partners, full, share, row):
    parts = refs[:partners]
    weight, out, mixed = refs[partners:]
    part = mixed.shape[0]
    for m in range(partners):
        chip = t_ref[0] ^ m
        for i in range(full):
            lane = pl.ds(pl.multiple_of((chip * full + i) * HD, HD), HD)
            mixed[:, lane] = parts[m][pl.ds(i * part, part)]
        lane = pl.ds(pl.multiple_of((partners * full + chip // share) * HD, HD), HD)
        rows = pl.ds(pl.multiple_of((chip % share) * row, 16), row)
        mixed[rows, lane] = parts[m][pl.ds(full * part, row)]
    shares, _, block = out.shape
    for d in range(shares):
        product = jnp.dot(mixed[...], weight[:, d * block : (d + 1) * block], preferred_element_type=jnp.float32)
        out[d] = product.astype(out.dtype)


def project(t, parts, weight, shares, full, share, row):
    partners = len(parts)
    feats, width = weight.shape
    part = (parts[0].shape[0] - row) // full
    block = width // shares
    whole = pl.BlockSpec(memory_space=pltpu.VMEM)

    def kernel(*refs):
        project_kernel(*refs, partners=partners, full=full, share=share, row=row)

    return pl.pallas_call(
        kernel,
        out_shape=jax.ShapeDtypeStruct((shares, part, block), jnp.bfloat16),
        in_specs=[pl.BlockSpec(memory_space=pltpu.SMEM)] + [whole] * (partners + 1),
        out_specs=whole,
        scratch_shapes=[pltpu.VMEM((part, feats), jnp.bfloat16)],
        compiler_params=VMEM,
        cost_estimate=pl.CostEstimate(
            flops=2 * part * feats * width, bytes_accessed=2 * feats * width, transcendentals=0
        ),
        name="project",
    )(t, *parts, weight)


def scatter_sums(chunks, axis):
    size = lax.axis_size(axis)
    place = lax.axis_index(axis)

    def share(mixed, d):
        return lax.dynamic_index_in_dim(mixed, jnp.clip(d, 0, size - 1), 0, False)

    held = [None] * len(chunks)
    for step in range(1, size):
        for c, mixed in enumerate(chunks):
            right = share(mixed, place + size - step)
            left = share(mixed, place - size + step)
            if held[c] is not None:
                right, left = right + held[c][0], left + held[c][1]
            right, left = lax.optimization_barrier((right, left))
            held[c] = (
                lax.ppermute(right, axis, [(i, i + 1) for i in range(step)]),
                lax.ppermute(left, axis, [(size - 1 - i, size - 2 - i) for i in range(step)]),
            )
    return [share(mixed, place) + right + left for mixed, (right, left) in zip(chunks, held)]


def exchange_plan(query, key, value, window, out_weight):
    frames_dev, rows_dev, width, feats = query.shape
    partners = lax.axis_size("tm")
    heads = feats // HD
    full = heads // partners
    share = partners // (heads - full * partners)
    t = lax.axis_index("tm").astype(jnp.int32)
    s = lax.axis_index("space").astype(jnp.int32)
    place = jnp.stack([t, s])
    tokens = rows_dev * width
    flat = [a.reshape(tokens, feats) for a in (query, key, value)]

    def swap(x, m):
        return x if m == 0 else lax.ppermute(x, "tm", [(i, i ^ m) for i in range(partners)])

    packed = [pack(place, *flat, m, partners, full, share, width) for m in range(partners)]
    near = [swap(p[0], m) for m, p in enumerate(packed)]
    far = [lax.ppermute(x, "space", [(0, 1), (1, 0)]) for x in near]

    mixed = []
    for c in range(CHUNKS):
        queries = near if c == 0 else [swap(p[c], m) for m, p in enumerate(packed)]
        done = attend(place, window, queries, near, far, c, full, share, width, rows_dev)
        done = [swap(x, m) for m, x in enumerate(done)]
        mixed.append(project(place, done, out_weight, lax.axis_size("head"), full, share, width))
    outputs = scatter_sums(mixed, "head")
    return jnp.concatenate(outputs, axis=0).reshape(frames_dev, rows_dev, width, -1)


def can_exchange(mesh, query, key, value, window, out_weight):
    partners, sides = mesh.shape["tm"], mesh.shape["space"]
    frames, rows, width, feats = query.shape
    heads = feats // HD // mesh.shape["head"]
    rows_dev = rows // sides
    rest = heads % partners
    if partners & (partners - 1) or sides != 2 or frames != partners or rest == 0 or heads < partners:
        return False
    return partners % rest == 0 and rows_dev == CHUNKS * (partners // rest) and width % 16 == 0


def padded_2(x, sides, width):
    for axis, dim in sides:
        size, length = (lax.axis_size(axis), x.shape[dim])
        up = [(i, (i + 1) % size) for i in range(size - 1)]
        down = [(j, i) for i, j in up]
        last = lax.slice_in_dim(x, length - width, length, axis=dim)
        first = lax.slice_in_dim(x, 0, width, axis=dim)
        before = lax.ppermute(last, axis, up)
        after = lax.ppermute(first, axis, down)
        x = jnp.concatenate([before, x, after], axis=dim)
    return x


def frame_mask(widths, query_rows, key_rows, total_rows, width):
    count = widths.shape[0]
    distance = jnp.abs(query_rows[:, None] - key_rows[None, :])
    inside_grid = (key_rows >= 0) & (key_rows < total_rows)
    inside = (
        (widths[:, None, None] >= 0)
        & (distance[None] <= widths[:, None, None])
        & inside_grid[None, None, :]
    )
    span_rows = key_rows.shape[0]
    full = jnp.broadcast_to(
        inside[:, :, None, :, None], (count, query_rows.shape[0], width, span_rows, width)
    )
    return full.reshape(count * query_rows.shape[0] * width, span_rows * width)


def absorb(state, queries, keys, values, mask):
    run_max, run_sum, run_acc = state
    scale = 1.0 / math.sqrt(HD)
    scores = jnp.einsum("qhd,khd->hqk", queries, keys, preferred_element_type=jnp.float32) * scale
    new_max = jnp.maximum(run_max, jnp.max(jnp.where(mask[None], scores, NEG_FILL), axis=-1))
    weights = jnp.where(mask[None], jnp.exp(scores - new_max[..., None]), 0.0)
    factor = jnp.exp(run_max - new_max)
    new_sum = run_sum * factor + jnp.sum(weights, axis=-1)
    new_acc = run_acc * factor[..., None] + jnp.einsum(
        "hqk,khd->hqd", weights.astype(jnp.bfloat16), values, preferred_element_type=jnp.float32
    )
    return (new_max, new_sum, new_acc)


def absorb_frame(state, queries, widths, kv_frame, query_rows, key_rows, total_rows):
    span_rows, width, feats = (kv_frame.shape[1], kv_frame.shape[2], kv_frame.shape[3])
    heads_dev = feats // HD
    keys = kv_frame[0].reshape(span_rows * width, heads_dev, HD)
    values = kv_frame[1].reshape(span_rows * width, heads_dev, HD)
    mask = frame_mask(widths, query_rows, key_rows, total_rows, width)
    return absorb(state, queries, keys, values, mask)


def empty_state(heads_dev, count):
    return (
        jnp.full((heads_dev, count), NEG_FILL, jnp.float32),
        jnp.zeros((heads_dev, count), jnp.float32),
        jnp.zeros((heads_dev, count, HD), jnp.float32),
    )


def gather_plan(query, key, value, window, out_weight):
    frames_dev, rows_dev, width, feats = query.shape
    heads_dev = feats // HD
    qcount = frames_dev * rows_dev * width
    total_rows = rows_dev * lax.axis_size("space")
    first_row = lax.axis_index("space") * rows_dev
    first_frame = lax.axis_index("tm") * frames_dev
    query_rows = first_row + jnp.arange(rows_dev, dtype=jnp.int32)
    stacked = jnp.stack([key, value])
    padded = padded_2(stacked, (("space", 2),), HALO)
    key_rows = first_row - HALO + jnp.arange(rows_dev + 2 * HALO, dtype=jnp.int32)
    my_windows = lax.dynamic_slice_in_dim(window, first_frame, frames_dev, 0)
    queries = query.reshape(qcount, heads_dev, HD)
    piece = lax.all_gather(padded, "tm", axis=1, tiled=True)

    def one_frame(carry, offset):
        kv_frame = lax.dynamic_index_in_dim(piece, offset, 1, False)
        widths = lax.dynamic_index_in_dim(my_windows, offset, 1, False)
        return (
            absorb_frame(carry, queries, widths, kv_frame, query_rows, key_rows, total_rows),
            None,
        )

    result, unused = lax.scan(
        one_frame, empty_state(heads_dev, qcount), jnp.arange(piece.shape[1], dtype=jnp.int32)
    )
    run_max, run_sum, run_acc = result
    attended = (
        (run_acc / run_sum[..., None])
        .transpose(1, 0, 2)
        .reshape(qcount, feats)
        .astype(jnp.bfloat16)
    )
    share_rows = out_weight.shape[1] // lax.axis_size("head")
    mixed = lax.psum_scatter(
        lax.dot_general(
            out_weight, attended, (((0,), (1,)), ((), ())), preferred_element_type=jnp.float32
        ).astype(jnp.bfloat16),
        "head",
        scatter_dimension=0,
        tiled=True,
    ).astype(jnp.float32)
    return mixed.T.reshape(frames_dev, rows_dev, width, share_rows).astype(jnp.bfloat16)


def solution(mesh):
    placed = (
        P("tm", "space", None, "head"),
        P("tm", "space", None, "head"),
        P("tm", "space", None, "head"),
        P(),
        P("head", None),
    )

    def run(*args):
        body = exchange_plan if can_exchange(mesh, *args) else gather_plan
        return jax.shard_map(
            body, mesh=mesh, in_specs=placed, out_specs=P("tm", "space", None, "head"), check_vma=False
        )(*args)

    return run
```

```python
import math

import jax
import jax.numpy as jnp
from jax import lax
from jax.experimental import pallas as pl
from jax.experimental.pallas import tpu as pltpu
from jax.sharding import PartitionSpec as P

HD = 128
HALO = 4
NEG_FILL = -1e30
CHUNKS = 2
VMEM = pltpu.CompilerParams(vmem_limit_bytes=32 * 1024 * 1024)


def pack_kernel(q_ref, k_ref, v_ref, first, *rest, partner, partners, full, share, row):
    sems = rest[-1]
    tokens = q_ref.shape[0]
    part = tokens // CHUNKS
    chip = lax.axis_index("tm") ^ partner
    heads = [chip * full + i for i in range(full)] + [partners * full + chip // share]
    lanes = [pl.ds(pl.multiple_of(h * HD, HD), HD) for h in heads]
    moves = []
    for kind, source in enumerate((k_ref, v_ref)):
        for i, lane in enumerate(lanes):
            place = pl.ds((kind * (full + 1) + i) * tokens, tokens)
            moves.append((source.at[:, lane], first.at[place]))
    for c in range(CHUNKS):
        target, base = (first, 2 * (full + 1) * tokens) if c == 0 else (rest[c - 1], 0)
        for i in range(full):
            moves.append((q_ref.at[pl.ds(c * part, part), lanes[i]], target.at[pl.ds(base + i * part, part)]))
        start = pl.multiple_of(c * part + (chip % share) * row, 16)
        moves.append((q_ref.at[pl.ds(start, row), lanes[full]], target.at[pl.ds(base + full * part, row)]))
    copies = [pltpu.make_async_copy(a, b, sems.at[n]) for n, (a, b) in enumerate(moves)]
    for copy in copies:
        copy.start()
    for copy in copies:
        copy.wait()


def pack(q, k, v, partner, partners, full, share, row):
    direct = partner == partners - 1
    tokens = q.shape[0]
    queries = full * (tokens // CHUNKS) + row
    slabs = 2 * (full + 1) * tokens + queries
    whole = pl.BlockSpec(memory_space=pltpu.VMEM)
    anywhere = pl.BlockSpec(memory_space=pl.ANY)
    shapes = [jax.ShapeDtypeStruct((slabs, HD), q.dtype)]
    shapes += [jax.ShapeDtypeStruct((queries, HD), q.dtype)] * (CHUNKS - 1)

    def kernel(*refs):
        pack_kernel(*refs, partner=partner, partners=partners, full=full, share=share, row=row)

    return pl.pallas_call(
        kernel,
        out_shape=shapes,
        in_specs=[anywhere] * 3,
        out_specs=[whole] * len(shapes),
        scratch_shapes=[pltpu.SemaphoreType.DMA(((full + 1) * (2 + CHUNKS),))],
        compiler_params=pltpu.CompilerParams(vmem_limit_bytes=(60 if direct else 32) * 1024 * 1024),
        name="pack",
    )(q, k, v)


def attend_kernel(
    window_ref, *refs, chunk, partners, full, share, row, rows_dev, total_rows, asked
):
    queries = refs[:partners]
    near = refs[partners : 2 * partners]
    far = refs[2 * partners : 3 * partners]
    outs = refs[3 * partners :]
    slots = full + 1
    tokens = rows_dev * row
    count = 2 * partners * tokens
    t, s = lax.axis_index("tm"), lax.axis_index("space")
    rows_part = rows_dev // CHUNKS
    factor = math.log2(math.e) / math.sqrt(HD)

    at = lax.broadcasted_iota(jnp.int32, (1, count), 1)
    frame = at // (2 * tokens)
    side = (at // tokens) % 2
    key_row = (at % tokens) // row + rows_dev * jnp.where(side == 0, s, 1 - s)
    widths = []
    for m in range(partners):
        wide = jnp.zeros_like(at)
        for m2 in range(partners):
            wide = jnp.where(frame == m2, window_ref[t ^ m, t ^ m2], wide)
        widths.append(wide)

    def bias(unit, m):
        part_row = unit % rows_part if unit < full * rows_part else t % share
        distance = jnp.abs(key_row - (rows_dev * s + rows_part * chunk + part_row))
        return jnp.where(distance <= widths[m], 0.0, NEG_FILL).astype(jnp.float32)

    def block(kind, slot):
        base = (kind * slots + slot) * tokens
        return jnp.concatenate([r[pl.ds(base, tokens)] for m in range(partners) for r in (near[m], far[m])], axis=0)

    def score(tile):
        unit, pair = tile
        q = jnp.concatenate([queries[m][pl.ds(asked + unit * row, row)] for m in pair], axis=0)
        return lax.dot_general(
            q, block(0, unit // rows_part), (((1,), (1,)), ((), ())), preferred_element_type=jnp.float32
        )

    def weigh(tile, scores):
        unit, pair = tile
        scores = jnp.concatenate(
            [scores[i * row : (i + 1) * row] + bias(unit, m) for i, m in enumerate(pair)], axis=0
        )
        top = jnp.max(scores, axis=-1, keepdims=True)
        return jnp.exp2((scores - top) * factor).astype(jnp.bfloat16)

    def gather(tile, weights):
        unit, pair = tile
        held = block(1, unit // rows_part)
        held = jnp.concatenate([held, jnp.ones_like(held)], axis=1)
        summed = jnp.dot(weights, held, preferred_element_type=jnp.float32)
        out = (summed[:, :HD] / summed[:, HD:]).astype(jnp.bfloat16)
        for i, m in enumerate(pair):
            outs[m][pl.ds(unit * row, row)] = out[i * row : (i + 1) * row]

    pairs = [tuple(range(m, m + 2)) for m in range(0, partners, 2)]
    tiles = [(unit, pair) for unit in range(full * rows_part + 1) for pair in pairs]
    scores, last = score(tiles[0]), None
    for i, tile in enumerate(tiles):
        following = score(tiles[i + 1]) if i + 1 < len(tiles) else None
        if last is not None:
            gather(*last)
        last = (tile, weigh(tile, scores))
        scores = following
    gather(*last)


def attend(window, queries, near, far, chunk, full, share, row, rows_dev):
    partners = len(queries)
    rows_out = full * (rows_dev // CHUNKS) * row + row
    count = 2 * partners * rows_dev * row
    whole = pl.BlockSpec(memory_space=pltpu.VMEM)
    scalars = pl.BlockSpec(memory_space=pltpu.SMEM)

    def kernel(*refs):
        attend_kernel(
            *refs,
            chunk=chunk,
            partners=partners,
            full=full,
            share=share,
            row=row,
            rows_dev=rows_dev,
            total_rows=2 * rows_dev,
            asked=queries[0].shape[0] - rows_out,
        )

    work = partners * rows_out * count
    return pl.pallas_call(
        kernel,
        out_shape=[jax.ShapeDtypeStruct((rows_out, HD), jnp.bfloat16)] * partners,
        in_specs=[scalars] + [whole] * (3 * partners),
        out_specs=[whole] * partners,
        compiler_params=VMEM,
        cost_estimate=pl.CostEstimate(
            flops=work * HD * 4, bytes_accessed=count * HD * 4 * (full + 1), transcendentals=work
        ),
        name="attend",
    )(window, *queries, *near, *far)


def shares_sent(place, size):
    wanted = []
    for k in range(1, size):
        right, left = place + size - k, place - size + k
        if 2 * k <= size:
            wanted.append(jnp.where(place < k, right, jnp.maximum(left, 0)))
        else:
            wanted += [jnp.minimum(right, size - 1), jnp.maximum(left, 0)]
    return [*wanted, place]


def project_kernel(*refs, after, partners, full, share, row, size):
    parts, weight, outs, mixed = refs[:partners], refs[partners], refs[partners + 1 + after : -1], refs[-1]
    part, block = outs[0].shape
    wide = full * HD
    t = lax.axis_index("tm")
    firsts, lasts = [], []
    for m in range(partners):
        for i in range(full):
            mixed[:, m * wide + i * HD : m * wide + (i + 1) * HD] = parts[m][pl.ds(i * part, part)]
        firsts.append((t ^ m) * wide)
        group, offset = divmod(m, share)
        lane = partners * wide + group * HD
        rows = pl.ds(pl.multiple_of((t ^ m) % share * row, 16), row)
        mixed[rows, lane : lane + HD] = parts[m][pl.ds(full * part, row)]
        if offset == 0:
            lasts.append(partners * wide + (t ^ m) // share * HD)
    starts = [(start, wide) for start in firsts] + [(start, HD) for start in lasts]
    for d, out in zip(shares_sent(lax.axis_index("head"), size), outs):
        columns = pl.ds(pl.multiple_of(d * block, HD), block)
        rows = [weight[pl.ds(pl.multiple_of(start, HD), n), columns] for start, n in starts]
        product = jnp.dot(mixed[...], jnp.concatenate(rows, axis=0), preferred_element_type=jnp.float32)
        out[...] = product.astype(out.dtype)


def project(parts, weight, size, full, share, row, after=()):
    partners = len(parts)
    feats, width = weight.shape
    part = (parts[0].shape[0] - row) // full
    count = len(shares_sent(0, size))
    whole = pl.BlockSpec(memory_space=pltpu.VMEM)

    def kernel(*refs):
        project_kernel(
            *refs, after=len(after), partners=partners, full=full, share=share, row=row, size=size
        )

    return pl.pallas_call(
        kernel,
        out_shape=[jax.ShapeDtypeStruct((part, width // size), jnp.bfloat16)] * count,
        in_specs=[whole] * (partners + 1) + [pl.BlockSpec(memory_space=pl.ANY)] * len(after),
        out_specs=[whole] * count,
        scratch_shapes=[pltpu.VMEM((part, feats), jnp.bfloat16)],
        compiler_params=VMEM,
        cost_estimate=pl.CostEstimate(
            flops=2 * part * feats * width, bytes_accessed=2 * feats * width, transcendentals=0
        ),
        name="project",
    )(*parts, weight, *after)


def begin_sums(shares, axis):
    size = lax.axis_size(axis)
    come = lax.ppermute(shares[0], axis, [(0, 1), (size - 1, size - 2)])
    return shares[1] + come, list(shares[2:])


def finish_sums(begun, axis):
    size = lax.axis_size(axis)
    held = [(sent, sent) for sent, _ in begun]
    for step in range(2, size):
        for c, (_, shares) in enumerate(begun):
            right, left = held[c]
            if step > 2:
                send_right = shares.pop(0)
                send_left = send_right if 2 * step <= size else shares.pop(0)
                right, left = send_right + right, send_left + left
            held[c] = (
                lax.ppermute(right, axis, [(i, i + 1) for i in range(step)]),
                lax.ppermute(left, axis, [(size - 1 - i, size - 2 - i) for i in range(step)]),
            )
    return [own + right + left for (_, (own,)), (right, left) in zip(begun, held)]


def exchange_plan(query, key, value, window, out_weight):
    frames_dev, rows_dev, width, feats = query.shape
    partners = lax.axis_size("tm")
    heads = feats // HD
    full = heads // partners
    share = partners // (heads - full * partners)
    tokens = rows_dev * width
    flat = [a.reshape(tokens, feats) for a in (query, key, value)]

    def swap(x, m):
        return x if m == 0 else lax.ppermute(x, "tm", [(i, i ^ m) for i in range(partners)])

    packed = [pack(*flat, m, partners, full, share, width) for m in range(partners)]
    near = [swap(p[0], m) for m, p in enumerate(packed)]
    far = [lax.ppermute(x, "space", [(0, 1), (1, 0)]) for x in near]

    done = []
    for c in range(CHUNKS):
        queries = near if c == 0 else [swap(p[c], m) for m, p in enumerate(packed)]
        done.append(attend(window, queries, near, far, c, full, share, width, rows_dev))
    begun = []
    for c in range(CHUNKS):
        parts = [swap(x, m) for m, x in enumerate(done[c])]
        after = [x[0] for x in done[c + 1 :]]
        shares = project(parts, out_weight, lax.axis_size("head"), full, share, width, after)
        begun.append(begin_sums(shares, "head"))
    outputs = finish_sums(begun, "head")
    return jnp.concatenate(outputs, axis=0).reshape(frames_dev, rows_dev, width, -1)


def can_exchange(mesh, query, key, value, window, out_weight):
    partners, sides = mesh.shape["tm"], mesh.shape["space"]
    frames, rows, width, feats = query.shape
    heads = feats // HD // mesh.shape["head"]
    rows_dev = rows // sides
    if mesh.shape["head"] != 4:
        return False
    rest = heads % partners
    if partners & (partners - 1) or sides != 2 or frames != partners or rest == 0 or heads < partners:
        return False
    return partners % rest == 0 and rows_dev == CHUNKS * (partners // rest) and width % 16 == 0


def padded_2(x, sides, width):
    for axis, dim in sides:
        size, length = (lax.axis_size(axis), x.shape[dim])
        up = [(i, (i + 1) % size) for i in range(size - 1)]
        down = [(j, i) for i, j in up]
        last = lax.slice_in_dim(x, length - width, length, axis=dim)
        first = lax.slice_in_dim(x, 0, width, axis=dim)
        before = lax.ppermute(last, axis, up)
        after = lax.ppermute(first, axis, down)
        x = jnp.concatenate([before, x, after], axis=dim)
    return x


def frame_mask(widths, query_rows, key_rows, total_rows, width):
    count = widths.shape[0]
    distance = jnp.abs(query_rows[:, None] - key_rows[None, :])
    inside_grid = (key_rows >= 0) & (key_rows < total_rows)
    inside = (
        (widths[:, None, None] >= 0)
        & (distance[None] <= widths[:, None, None])
        & inside_grid[None, None, :]
    )
    span_rows = key_rows.shape[0]
    full = jnp.broadcast_to(
        inside[:, :, None, :, None], (count, query_rows.shape[0], width, span_rows, width)
    )
    return full.reshape(count * query_rows.shape[0] * width, span_rows * width)


def absorb(state, queries, keys, values, mask):
    run_max, run_sum, run_acc = state
    scale = 1.0 / math.sqrt(HD)
    scores = jnp.einsum("qhd,khd->hqk", queries, keys, preferred_element_type=jnp.float32) * scale
    new_max = jnp.maximum(run_max, jnp.max(jnp.where(mask[None], scores, NEG_FILL), axis=-1))
    weights = jnp.where(mask[None], jnp.exp(scores - new_max[..., None]), 0.0)
    factor = jnp.exp(run_max - new_max)
    new_sum = run_sum * factor + jnp.sum(weights, axis=-1)
    new_acc = run_acc * factor[..., None] + jnp.einsum(
        "hqk,khd->hqd", weights.astype(jnp.bfloat16), values, preferred_element_type=jnp.float32
    )
    return (new_max, new_sum, new_acc)


def absorb_frame(state, queries, widths, kv_frame, query_rows, key_rows, total_rows):
    span_rows, width, feats = (kv_frame.shape[1], kv_frame.shape[2], kv_frame.shape[3])
    heads_dev = feats // HD
    keys = kv_frame[0].reshape(span_rows * width, heads_dev, HD)
    values = kv_frame[1].reshape(span_rows * width, heads_dev, HD)
    mask = frame_mask(widths, query_rows, key_rows, total_rows, width)
    return absorb(state, queries, keys, values, mask)


def empty_state(heads_dev, count):
    return (
        jnp.full((heads_dev, count), NEG_FILL, jnp.float32),
        jnp.zeros((heads_dev, count), jnp.float32),
        jnp.zeros((heads_dev, count, HD), jnp.float32),
    )


def gather_plan(query, key, value, window, out_weight):
    frames_dev, rows_dev, width, feats = query.shape
    heads_dev = feats // HD
    qcount = frames_dev * rows_dev * width
    total_rows = rows_dev * lax.axis_size("space")
    first_row = lax.axis_index("space") * rows_dev
    first_frame = lax.axis_index("tm") * frames_dev
    query_rows = first_row + jnp.arange(rows_dev, dtype=jnp.int32)
    stacked = jnp.stack([key, value])
    padded = padded_2(stacked, (("space", 2),), HALO)
    key_rows = first_row - HALO + jnp.arange(rows_dev + 2 * HALO, dtype=jnp.int32)
    my_windows = lax.dynamic_slice_in_dim(window, first_frame, frames_dev, 0)
    queries = query.reshape(qcount, heads_dev, HD)
    piece = lax.all_gather(padded, "tm", axis=1, tiled=True)

    def one_frame(carry, offset):
        kv_frame = lax.dynamic_index_in_dim(piece, offset, 1, False)
        widths = lax.dynamic_index_in_dim(my_windows, offset, 1, False)
        return (
            absorb_frame(carry, queries, widths, kv_frame, query_rows, key_rows, total_rows),
            None,
        )

    result, unused = lax.scan(
        one_frame, empty_state(heads_dev, qcount), jnp.arange(piece.shape[1], dtype=jnp.int32)
    )
    run_max, run_sum, run_acc = result
    attended = (
        (run_acc / run_sum[..., None])
        .transpose(1, 0, 2)
        .reshape(qcount, feats)
        .astype(jnp.bfloat16)
    )
    share_rows = out_weight.shape[1] // lax.axis_size("head")
    mixed = lax.psum_scatter(
        lax.dot_general(
            out_weight, attended, (((0,), (1,)), ((), ())), preferred_element_type=jnp.float32
        ).astype(jnp.bfloat16),
        "head",
        scatter_dimension=0,
        tiled=True,
    ).astype(jnp.float32)
    return mixed.T.reshape(frames_dev, rows_dev, width, share_rows).astype(jnp.bfloat16)


def solution(mesh):
    placed = (
        P("tm", "space", None, "head"),
        P("tm", "space", None, "head"),
        P("tm", "space", None, "head"),
        P(),
        P("head", None),
    )

    def run(*args):
        body = exchange_plan if can_exchange(mesh, *args) else gather_plan
        return jax.shard_map(
            body, mesh=mesh, in_specs=placed, out_specs=P("tm", "space", None, "head"), check_vma=False
        )(*args)

    return run
```

```python
import math

import jax
import jax.numpy as jnp
from jax import lax
from jax.experimental import pallas as pl
from jax.experimental.pallas import tpu as pltpu
from jax.sharding import PartitionSpec as P

HD = 128
HALO = 4
NEG_FILL = -1e30
CHUNKS = 2
VMEM = pltpu.CompilerParams(vmem_limit_bytes=32 * 1024 * 1024)


def pack_kernel(q_ref, k_ref, v_ref, first, *rest, partner, partners, full, share, row):
    sems = rest[-1]
    tokens = q_ref.shape[0]
    part = tokens // CHUNKS
    chip = lax.axis_index("tm") ^ partner
    heads = [chip * full + i for i in range(full)] + [partners * full + chip // share]
    lanes = [pl.ds(pl.multiple_of(h * HD, HD), HD) for h in heads]
    moves = []
    for kind, source in enumerate((k_ref, v_ref)):
        for i, lane in enumerate(lanes):
            place = pl.ds((kind * (full + 1) + i) * tokens, tokens)
            moves.append((source.at[:, lane], first.at[place]))
    for c in range(CHUNKS):
        target, base = (first, 2 * (full + 1) * tokens) if c == 0 else (rest[c - 1], 0)
        for i in range(full):
            moves.append((q_ref.at[pl.ds(c * part, part), lanes[i]], target.at[pl.ds(base + i * part, part)]))
        start = pl.multiple_of(c * part + (chip % share) * row, 16)
        moves.append((q_ref.at[pl.ds(start, row), lanes[full]], target.at[pl.ds(base + full * part, row)]))
    copies = [pltpu.make_async_copy(a, b, sems.at[n]) for n, (a, b) in enumerate(moves)]
    for copy in copies:
        copy.start()
    for copy in copies:
        copy.wait()


def pack(q, k, v, partner, partners, full, share, row):
    direct = partner == partners - 1
    tokens = q.shape[0]
    queries = full * (tokens // CHUNKS) + row
    slabs = 2 * (full + 1) * tokens + queries
    whole = pl.BlockSpec(memory_space=pltpu.VMEM)
    anywhere = pl.BlockSpec(memory_space=pl.ANY)
    shapes = [jax.ShapeDtypeStruct((slabs, HD), q.dtype)]
    shapes += [jax.ShapeDtypeStruct((queries, HD), q.dtype)] * (CHUNKS - 1)

    def kernel(*refs):
        pack_kernel(*refs, partner=partner, partners=partners, full=full, share=share, row=row)

    return pl.pallas_call(
        kernel,
        out_shape=shapes,
        in_specs=[anywhere] * 3,
        out_specs=[whole] * len(shapes),
        scratch_shapes=[pltpu.SemaphoreType.DMA(((full + 1) * (2 + CHUNKS),))],
        compiler_params=pltpu.CompilerParams(vmem_limit_bytes=(60 if direct else 32) * 1024 * 1024),
        name="pack",
    )(q, k, v)


def attend_kernel(
    window_ref, *refs, chunk, partners, full, share, row, rows_dev, total_rows, asked
):
    queries = refs[:partners]
    near = refs[partners : 2 * partners]
    far = refs[2 * partners : 3 * partners]
    outs = refs[3 * partners :]
    slots = full + 1
    tokens = rows_dev * row
    count = 2 * partners * tokens
    t, s = lax.axis_index("tm"), lax.axis_index("space")
    rows_part = rows_dev // CHUNKS
    factor = math.log2(math.e) / math.sqrt(HD)

    at = lax.broadcasted_iota(jnp.int32, (1, count), 1)
    frame = at // (2 * tokens)
    side = (at // tokens) % 2
    key_row = (at % tokens) // row + rows_dev * jnp.where(side == 0, s, 1 - s)
    widths = []
    for m in range(partners):
        wide = jnp.zeros_like(at)
        for m2 in range(partners):
            wide = jnp.where(frame == m2, window_ref[t ^ m, t ^ m2], wide)
        widths.append(wide)

    def bias(unit, m):
        part_row = unit % rows_part if unit < full * rows_part else t % share
        distance = jnp.abs(key_row - (rows_dev * s + rows_part * chunk + part_row))
        return jnp.where(distance <= widths[m], 0.0, NEG_FILL).astype(jnp.float32)

    def block(kind, slot):
        base = (kind * slots + slot) * tokens
        return jnp.concatenate([r[pl.ds(base, tokens)] for m in range(partners) for r in (near[m], far[m])], axis=0)

    def score(tile):
        unit, pair = tile
        q = jnp.concatenate([queries[m][pl.ds(asked + unit * row, row)] for m in pair], axis=0)
        return lax.dot_general(
            q, block(0, unit // rows_part), (((1,), (1,)), ((), ())), preferred_element_type=jnp.float32
        )

    def weigh(tile, scores):
        unit, pair = tile
        scores = jnp.concatenate(
            [scores[i * row : (i + 1) * row] + bias(unit, m) for i, m in enumerate(pair)], axis=0
        )
        top = jnp.max(scores, axis=-1, keepdims=True)
        return jnp.exp2((scores - top) * factor).astype(jnp.bfloat16)

    def gather(tile, weights):
        unit, pair = tile
        held = block(1, unit // rows_part)
        held = jnp.concatenate([held, jnp.ones_like(held)], axis=1)
        summed = jnp.dot(weights, held, preferred_element_type=jnp.float32)
        out = (summed[:, :HD] / summed[:, HD:]).astype(jnp.bfloat16)
        for i, m in enumerate(pair):
            outs[m][pl.ds(unit * row, row)] = out[i * row : (i + 1) * row]

    pairs = [tuple(range(m, m + 2)) for m in range(0, partners, 2)]
    tiles = [(unit, pair) for unit in range(full * rows_part + 1) for pair in pairs]
    scores, last = score(tiles[0]), None
    for i, tile in enumerate(tiles):
        following = score(tiles[i + 1]) if i + 1 < len(tiles) else None
        if last is not None:
            gather(*last)
        last = (tile, weigh(tile, scores))
        scores = following
    gather(*last)


def attend(window, queries, near, far, chunk, full, share, row, rows_dev):
    partners = len(queries)
    rows_out = full * (rows_dev // CHUNKS) * row + row
    count = 2 * partners * rows_dev * row
    whole = pl.BlockSpec(memory_space=pltpu.VMEM)
    scalars = pl.BlockSpec(memory_space=pltpu.SMEM)

    def kernel(*refs):
        attend_kernel(
            *refs,
            chunk=chunk,
            partners=partners,
            full=full,
            share=share,
            row=row,
            rows_dev=rows_dev,
            total_rows=2 * rows_dev,
            asked=queries[0].shape[0] - rows_out,
        )

    work = partners * rows_out * count
    return pl.pallas_call(
        kernel,
        out_shape=[jax.ShapeDtypeStruct((rows_out, HD), jnp.bfloat16)] * partners,
        in_specs=[scalars] + [whole] * (3 * partners),
        out_specs=[whole] * partners,
        compiler_params=VMEM,
        cost_estimate=pl.CostEstimate(
            flops=work * HD * 4, bytes_accessed=count * HD * 4 * (full + 1), transcendentals=work
        ),
        name="attend",
    )(window, *queries, *near, *far)


def shares_sent(place, size):
    wanted = []
    for k in range(1, size):
        right, left = place + size - k, place - size + k
        if 2 * k <= size:
            wanted.append(jnp.where(place < k, right, jnp.maximum(left, 0)))
        else:
            wanted += [jnp.minimum(right, size - 1), jnp.maximum(left, 0)]
    return [*wanted, place]


def project_kernel(*refs, after, partners, full, share, row, size, chosen):
    parts, weight, outs, mixed = refs[:partners], refs[partners], refs[partners + 1 + after : -1], refs[-1]
    part, block = outs[0].shape
    wide = full * HD
    t = lax.axis_index("tm")
    firsts, lasts = [], []
    for m in range(partners):
        for i in range(full):
            mixed[:, m * wide + i * HD : m * wide + (i + 1) * HD] = parts[m][pl.ds(i * part, part)]
        firsts.append((t ^ m) * wide)
        group, offset = divmod(m, share)
        lane = partners * wide + group * HD
        rows = pl.ds(pl.multiple_of((t ^ m) % share * row, 16), row)
        mixed[rows, lane : lane + HD] = parts[m][pl.ds(full * part, row)]
        if offset == 0:
            lasts.append(partners * wide + (t ^ m) // share * HD)
    starts = [(start, wide) for start in firsts] + [(start, HD) for start in lasts]
    for d, out in zip(shares_sent(lax.axis_index("head"), size)[chosen], outs):
        columns = pl.ds(pl.multiple_of(d * block, HD), block)
        rows = [weight[pl.ds(pl.multiple_of(start, HD), n), columns] for start, n in starts]
        product = jnp.dot(mixed[...], jnp.concatenate(rows, axis=0), preferred_element_type=jnp.float32)
        out[...] = product.astype(out.dtype)


def project(parts, weight, size, full, share, row, chosen, after=()):
    partners = len(parts)
    feats, width = weight.shape
    part = (parts[0].shape[0] - row) // full
    count = len(shares_sent(0, size)[chosen])
    whole = pl.BlockSpec(memory_space=pltpu.VMEM)

    def kernel(*refs):
        project_kernel(
            *refs,
            after=len(after),
            partners=partners,
            full=full,
            share=share,
            row=row,
            size=size,
            chosen=chosen,
        )

    return pl.pallas_call(
        kernel,
        out_shape=[jax.ShapeDtypeStruct((part, width // size), jnp.bfloat16)] * count,
        in_specs=[whole] * (partners + 1) + [pl.BlockSpec(memory_space=pl.ANY)] * len(after),
        out_specs=[whole] * count,
        scratch_shapes=[pltpu.VMEM((part, feats), jnp.bfloat16)],
        compiler_params=VMEM,
        cost_estimate=pl.CostEstimate(
            flops=2 * part * feats * width, bytes_accessed=2 * feats * width, transcendentals=0
        ),
        name="project",
    )(*parts, weight, *after)


def begin_sums(shares, axis):
    size = lax.axis_size(axis)
    come = lax.ppermute(shares[0], axis, [(0, 1), (size - 1, size - 2)])
    return shares[1] + come, list(shares[2:])


def finish_sums(begun, axis):
    size = lax.axis_size(axis)
    held = [(sent, sent) for sent, _ in begun]
    for step in range(2, size):
        for c, (_, shares) in enumerate(begun):
            right, left = held[c]
            if step > 2:
                send_right = shares.pop(0)
                send_left = send_right if 2 * step <= size else shares.pop(0)
                right, left = send_right + right, send_left + left
            held[c] = (
                lax.ppermute(right, axis, [(i, i + 1) for i in range(step)]),
                lax.ppermute(left, axis, [(size - 1 - i, size - 2 - i) for i in range(step)]),
            )
    return [own + right + left for (_, (own,)), (right, left) in zip(begun, held)]


def exchange_plan(query, key, value, window, out_weight):
    frames_dev, rows_dev, width, feats = query.shape
    partners = lax.axis_size("tm")
    heads = feats // HD
    full = heads // partners
    share = partners // (heads - full * partners)
    tokens = rows_dev * width
    flat = [a.reshape(tokens, feats) for a in (query, key, value)]

    def swap(x, m):
        return x if m == 0 else lax.ppermute(x, "tm", [(i, i ^ m) for i in range(partners)])

    packed = [pack(*flat, m, partners, full, share, width) for m in range(partners)]
    near = [swap(p[0], m) for m, p in enumerate(packed)]
    far = [lax.ppermute(x, "space", [(0, 1), (1, 0)]) for x in near]

    done = []
    for c in range(CHUNKS):
        queries = near if c == 0 else [swap(p[c], m) for m, p in enumerate(packed)]
        done.append(attend(window, queries, near, far, c, full, share, width, rows_dev))
    begun, shares = [], ()
    for c in range(CHUNKS):
        parts = [swap(x, m) for m, x in enumerate(done[c])]
        common = (parts, out_weight, lax.axis_size("head"), full, share, width)
        if c == 0:
            shares = project(*common, slice(1), [x[0] for x in done[1:]])
            shares += project(*common, slice(1, None))
        else:
            shares = project(*common, slice(1), shares[-1:])
            shares += project(*common, slice(1, None))
        begun.append(begin_sums(shares, "head"))
        if c == 0:
            first, *done[1] = lax.optimization_barrier((shares[0], *done[1]))
    outputs = finish_sums(begun, "head")
    return jnp.concatenate(outputs, axis=0).reshape(frames_dev, rows_dev, width, -1)


def can_exchange(mesh, query, key, value, window, out_weight):
    partners, sides = mesh.shape["tm"], mesh.shape["space"]
    frames, rows, width, feats = query.shape
    heads = feats // HD // mesh.shape["head"]
    rows_dev = rows // sides
    if mesh.shape["head"] != 4:
        return False
    rest = heads % partners
    if partners & (partners - 1) or sides != 2 or frames != partners or rest == 0 or heads < partners:
        return False
    return partners % rest == 0 and rows_dev == CHUNKS * (partners // rest) and width % 16 == 0


def padded_2(x, sides, width):
    for axis, dim in sides:
        size, length = (lax.axis_size(axis), x.shape[dim])
        up = [(i, (i + 1) % size) for i in range(size - 1)]
        down = [(j, i) for i, j in up]
        last = lax.slice_in_dim(x, length - width, length, axis=dim)
        first = lax.slice_in_dim(x, 0, width, axis=dim)
        before = lax.ppermute(last, axis, up)
        after = lax.ppermute(first, axis, down)
        x = jnp.concatenate([before, x, after], axis=dim)
    return x


def frame_mask(widths, query_rows, key_rows, total_rows, width):
    count = widths.shape[0]
    distance = jnp.abs(query_rows[:, None] - key_rows[None, :])
    inside_grid = (key_rows >= 0) & (key_rows < total_rows)
    inside = (
        (widths[:, None, None] >= 0)
        & (distance[None] <= widths[:, None, None])
        & inside_grid[None, None, :]
    )
    span_rows = key_rows.shape[0]
    full = jnp.broadcast_to(
        inside[:, :, None, :, None], (count, query_rows.shape[0], width, span_rows, width)
    )
    return full.reshape(count * query_rows.shape[0] * width, span_rows * width)


def absorb(state, queries, keys, values, mask):
    run_max, run_sum, run_acc = state
    scale = 1.0 / math.sqrt(HD)
    scores = jnp.einsum("qhd,khd->hqk", queries, keys, preferred_element_type=jnp.float32) * scale
    new_max = jnp.maximum(run_max, jnp.max(jnp.where(mask[None], scores, NEG_FILL), axis=-1))
    weights = jnp.where(mask[None], jnp.exp(scores - new_max[..., None]), 0.0)
    factor = jnp.exp(run_max - new_max)
    new_sum = run_sum * factor + jnp.sum(weights, axis=-1)
    new_acc = run_acc * factor[..., None] + jnp.einsum(
        "hqk,khd->hqd", weights.astype(jnp.bfloat16), values, preferred_element_type=jnp.float32
    )
    return (new_max, new_sum, new_acc)


def absorb_frame(state, queries, widths, kv_frame, query_rows, key_rows, total_rows):
    span_rows, width, feats = (kv_frame.shape[1], kv_frame.shape[2], kv_frame.shape[3])
    heads_dev = feats // HD
    keys = kv_frame[0].reshape(span_rows * width, heads_dev, HD)
    values = kv_frame[1].reshape(span_rows * width, heads_dev, HD)
    mask = frame_mask(widths, query_rows, key_rows, total_rows, width)
    return absorb(state, queries, keys, values, mask)


def empty_state(heads_dev, count):
    return (
        jnp.full((heads_dev, count), NEG_FILL, jnp.float32),
        jnp.zeros((heads_dev, count), jnp.float32),
        jnp.zeros((heads_dev, count, HD), jnp.float32),
    )


def gather_plan(query, key, value, window, out_weight):
    frames_dev, rows_dev, width, feats = query.shape
    heads_dev = feats // HD
    qcount = frames_dev * rows_dev * width
    total_rows = rows_dev * lax.axis_size("space")
    first_row = lax.axis_index("space") * rows_dev
    first_frame = lax.axis_index("tm") * frames_dev
    query_rows = first_row + jnp.arange(rows_dev, dtype=jnp.int32)
    stacked = jnp.stack([key, value])
    padded = padded_2(stacked, (("space", 2),), HALO)
    key_rows = first_row - HALO + jnp.arange(rows_dev + 2 * HALO, dtype=jnp.int32)
    my_windows = lax.dynamic_slice_in_dim(window, first_frame, frames_dev, 0)
    queries = query.reshape(qcount, heads_dev, HD)
    piece = lax.all_gather(padded, "tm", axis=1, tiled=True)

    def one_frame(carry, offset):
        kv_frame = lax.dynamic_index_in_dim(piece, offset, 1, False)
        widths = lax.dynamic_index_in_dim(my_windows, offset, 1, False)
        return (
            absorb_frame(carry, queries, widths, kv_frame, query_rows, key_rows, total_rows),
            None,
        )

    result, unused = lax.scan(
        one_frame, empty_state(heads_dev, qcount), jnp.arange(piece.shape[1], dtype=jnp.int32)
    )
    run_max, run_sum, run_acc = result
    attended = (
        (run_acc / run_sum[..., None])
        .transpose(1, 0, 2)
        .reshape(qcount, feats)
        .astype(jnp.bfloat16)
    )
    share_rows = out_weight.shape[1] // lax.axis_size("head")
    mixed = lax.psum_scatter(
        lax.dot_general(
            out_weight, attended, (((0,), (1,)), ((), ())), preferred_element_type=jnp.float32
        ).astype(jnp.bfloat16),
        "head",
        scatter_dimension=0,
        tiled=True,
    ).astype(jnp.float32)
    return mixed.T.reshape(frames_dev, rows_dev, width, share_rows).astype(jnp.bfloat16)


def solution(mesh):
    placed = (
        P("tm", "space", None, "head"),
        P("tm", "space", None, "head"),
        P("tm", "space", None, "head"),
        P(),
        P("head", None),
    )

    def run(*args):
        body = exchange_plan if can_exchange(mesh, *args) else gather_plan
        return jax.shard_map(
            body, mesh=mesh, in_specs=placed, out_specs=P("tm", "space", None, "head"), check_vma=False
        )(*args)

    return run
```

```python
import math

import jax
import jax.numpy as jnp
from jax import lax
from jax.experimental import pallas as pl
from jax.experimental.pallas import tpu as pltpu
from jax.sharding import PartitionSpec as P

HD = 128
HALO = 4
NEG_FILL = -1e30
CHUNKS = 2
VMEM = pltpu.CompilerParams(vmem_limit_bytes=32 * 1024 * 1024)


def pack_kernel(q_ref, k_ref, v_ref, first, *rest, partner, partners, full, share, row):
    sems = rest[-1]
    tokens = q_ref.shape[0]
    part = tokens // CHUNKS
    chip = lax.axis_index("tm") ^ partner
    heads = [chip * full + i for i in range(full)] + [partners * full + chip // share]
    lanes = [pl.ds(pl.multiple_of(h * HD, HD), HD) for h in heads]
    moves = []
    for kind, source in enumerate((k_ref, v_ref)):
        for i, lane in enumerate(lanes):
            place = pl.ds((kind * (full + 1) + i) * tokens, tokens)
            moves.append((source.at[:, lane], first.at[place]))
    for c in range(CHUNKS):
        target, base = (first, 2 * (full + 1) * tokens) if c == 0 else (rest[c - 1], 0)
        for i in range(full):
            moves.append((q_ref.at[pl.ds(c * part, part), lanes[i]], target.at[pl.ds(base + i * part, part)]))
        start = pl.multiple_of(c * part + (chip % share) * row, 16)
        moves.append((q_ref.at[pl.ds(start, row), lanes[full]], target.at[pl.ds(base + full * part, row)]))
    copies = [pltpu.make_async_copy(a, b, sems.at[n]) for n, (a, b) in enumerate(moves)]
    for copy in copies:
        copy.start()
    for copy in copies:
        copy.wait()


def pack(q, k, v, partner, partners, full, share, row):
    direct = partner == partners - 1
    tokens = q.shape[0]
    queries = full * (tokens // CHUNKS) + row
    slabs = 2 * (full + 1) * tokens + queries
    whole = pl.BlockSpec(memory_space=pltpu.VMEM)
    anywhere = pl.BlockSpec(memory_space=pl.ANY)
    shapes = [jax.ShapeDtypeStruct((slabs, HD), q.dtype)]
    shapes += [jax.ShapeDtypeStruct((queries, HD), q.dtype)] * (CHUNKS - 1)

    def kernel(*refs):
        pack_kernel(*refs, partner=partner, partners=partners, full=full, share=share, row=row)

    return pl.pallas_call(
        kernel,
        out_shape=shapes,
        in_specs=[anywhere] * 3,
        out_specs=[whole] * len(shapes),
        scratch_shapes=[pltpu.SemaphoreType.DMA(((full + 1) * (2 + CHUNKS),))],
        compiler_params=pltpu.CompilerParams(vmem_limit_bytes=(60 if direct else 32) * 1024 * 1024),
        name="pack",
    )(q, k, v)


def attend_kernel(
    window_ref, *refs, chunk, partners, full, share, row, rows_dev, total_rows, asked
):
    queries = refs[:partners]
    near = refs[partners : 2 * partners]
    far = refs[2 * partners : 3 * partners]
    outs = refs[3 * partners :]
    slots = full + 1
    tokens = rows_dev * row
    count = 2 * partners * tokens
    t, s = lax.axis_index("tm"), lax.axis_index("space")
    rows_part = rows_dev // CHUNKS
    factor = math.log2(math.e) / math.sqrt(HD)

    at = lax.broadcasted_iota(jnp.int32, (1, count), 1)
    frame = at // (2 * tokens)
    side = (at // tokens) % 2
    key_row = (at % tokens) // row + rows_dev * jnp.where(side == 0, s, 1 - s)
    widths = []
    for m in range(partners):
        wide = jnp.zeros_like(at)
        for m2 in range(partners):
            wide = jnp.where(frame == m2, window_ref[t ^ m, t ^ m2], wide)
        widths.append(wide)

    def bias(unit, m):
        part_row = unit % rows_part if unit < full * rows_part else t % share
        distance = jnp.abs(key_row - (rows_dev * s + rows_part * chunk + part_row))
        return jnp.where(distance <= widths[m], 0.0, NEG_FILL).astype(jnp.float32)

    def block(kind, slot):
        base = (kind * slots + slot) * tokens
        return jnp.concatenate([r[pl.ds(base, tokens)] for m in range(partners) for r in (near[m], far[m])], axis=0)

    def score(tile):
        unit, pair = tile
        q = jnp.concatenate([queries[m][pl.ds(asked + unit * row, row)] for m in pair], axis=0)
        return lax.dot_general(
            q, block(0, unit // rows_part), (((1,), (1,)), ((), ())), preferred_element_type=jnp.float32
        )

    def weigh(tile, scores):
        unit, pair = tile
        scores = jnp.concatenate(
            [scores[i * row : (i + 1) * row] + bias(unit, m) for i, m in enumerate(pair)], axis=0
        )
        top = jnp.max(scores, axis=-1, keepdims=True)
        return jnp.exp2((scores - top) * factor).astype(jnp.bfloat16)

    def gather(tile, weights):
        unit, pair = tile
        held = block(1, unit // rows_part)
        held = jnp.concatenate([held, jnp.ones_like(held)], axis=1)
        summed = jnp.dot(weights, held, preferred_element_type=jnp.float32)
        out = (summed[:, :HD] / summed[:, HD:]).astype(jnp.bfloat16)
        for i, m in enumerate(pair):
            outs[m][pl.ds(unit * row, row)] = out[i * row : (i + 1) * row]

    pairs = [tuple(range(m, m + 2)) for m in range(0, partners, 2)]
    tiles = [(unit, pair) for unit in range(full * rows_part + 1) for pair in pairs]
    scores, last = score(tiles[0]), None
    for i, tile in enumerate(tiles):
        if last is not None:
            gather(*last)
        following = score(tiles[i + 1]) if i + 1 < len(tiles) else None
        last = (tile, weigh(tile, scores))
        scores = following
    gather(*last)


def attend(window, queries, near, far, chunk, full, share, row, rows_dev):
    partners = len(queries)
    rows_out = full * (rows_dev // CHUNKS) * row + row
    count = 2 * partners * rows_dev * row
    whole = pl.BlockSpec(memory_space=pltpu.VMEM)
    scalars = pl.BlockSpec(memory_space=pltpu.SMEM)

    def kernel(*refs):
        attend_kernel(
            *refs,
            chunk=chunk,
            partners=partners,
            full=full,
            share=share,
            row=row,
            rows_dev=rows_dev,
            total_rows=2 * rows_dev,
            asked=queries[0].shape[0] - rows_out,
        )

    work = partners * rows_out * count
    return pl.pallas_call(
        kernel,
        out_shape=[jax.ShapeDtypeStruct((rows_out, HD), jnp.bfloat16)] * partners,
        in_specs=[scalars] + [whole] * (3 * partners),
        out_specs=[whole] * partners,
        compiler_params=VMEM,
        cost_estimate=pl.CostEstimate(
            flops=work * HD * 4, bytes_accessed=count * HD * 4 * (full + 1), transcendentals=work
        ),
        name="attend",
    )(window, *queries, *near, *far)


def shares_sent(place, size):
    wanted = []
    for k in range(1, size):
        right, left = place + size - k, place - size + k
        if 2 * k <= size:
            wanted.append(jnp.where(place < k, right, jnp.maximum(left, 0)))
        else:
            wanted += [jnp.minimum(right, size - 1), jnp.maximum(left, 0)]
    return [*wanted, place]


def project_kernel(*refs, after, partners, full, share, row, size, chosen):
    parts, weight, outs, mixed = refs[:partners], refs[partners], refs[partners + 1 + after : -1], refs[-1]
    part, block = outs[0].shape
    wide = full * HD
    t = lax.axis_index("tm")
    firsts, lasts = [], []
    for m in range(partners):
        for i in range(full):
            mixed[:, m * wide + i * HD : m * wide + (i + 1) * HD] = parts[m][pl.ds(i * part, part)]
        firsts.append((t ^ m) * wide)
        group, offset = divmod(m, share)
        lane = partners * wide + group * HD
        rows = pl.ds(pl.multiple_of((t ^ m) % share * row, 16), row)
        mixed[rows, lane : lane + HD] = parts[m][pl.ds(full * part, row)]
        if offset == 0:
            lasts.append(partners * wide + (t ^ m) // share * HD)
    starts = [(start, wide) for start in firsts] + [(start, HD) for start in lasts]
    for d, out in zip(shares_sent(lax.axis_index("head"), size)[chosen], outs):
        columns = pl.ds(pl.multiple_of(d * block, HD), block)
        rows = [weight[pl.ds(pl.multiple_of(start, HD), n), columns] for start, n in starts]
        product = jnp.dot(mixed[...], jnp.concatenate(rows, axis=0), preferred_element_type=jnp.float32)
        out[...] = product.astype(out.dtype)


def project(parts, weight, size, full, share, row, chosen, after=()):
    partners = len(parts)
    feats, width = weight.shape
    part = (parts[0].shape[0] - row) // full
    count = len(shares_sent(0, size)[chosen])
    whole = pl.BlockSpec(memory_space=pltpu.VMEM)

    def kernel(*refs):
        project_kernel(
            *refs,
            after=len(after),
            partners=partners,
            full=full,
            share=share,
            row=row,
            size=size,
            chosen=chosen,
        )

    return pl.pallas_call(
        kernel,
        out_shape=[jax.ShapeDtypeStruct((part, width // size), jnp.bfloat16)] * count,
        in_specs=[whole] * (partners + 1) + [pl.BlockSpec(memory_space=pl.ANY)] * len(after),
        out_specs=[whole] * count,
        scratch_shapes=[pltpu.VMEM((part, feats), jnp.bfloat16)],
        compiler_params=VMEM,
        cost_estimate=pl.CostEstimate(
            flops=2 * part * feats * width, bytes_accessed=2 * feats * width, transcendentals=0
        ),
        name="project",
    )(*parts, weight, *after)


def begin_sums(shares, axis):
    size = lax.axis_size(axis)
    come = lax.ppermute(shares[0], axis, [(0, 1), (size - 1, size - 2)])
    return shares[1] + come, list(shares[2:])


def finish_sums(begun, axis):
    size = lax.axis_size(axis)
    held = [(sent, sent) for sent, _ in begun]
    for step in range(2, size):
        for c, (_, shares) in enumerate(begun):
            right, left = held[c]
            if step > 2:
                send_right = shares.pop(0)
                send_left = send_right if 2 * step <= size else shares.pop(0)
                right, left = send_right + right, send_left + left
            held[c] = (
                lax.ppermute(right, axis, [(i, i + 1) for i in range(step)]),
                lax.ppermute(left, axis, [(size - 1 - i, size - 2 - i) for i in range(step)]),
            )
    return [own + right + left for (_, (own,)), (right, left) in zip(begun, held)]


def exchange_plan(query, key, value, window, out_weight):
    frames_dev, rows_dev, width, feats = query.shape
    partners = lax.axis_size("tm")
    heads = feats // HD
    full = heads // partners
    share = partners // (heads - full * partners)
    tokens = rows_dev * width
    flat = [a.reshape(tokens, feats) for a in (query, key, value)]

    def swap(x, m):
        return x if m == 0 else lax.ppermute(x, "tm", [(i, i ^ m) for i in range(partners)])

    packed = [pack(*flat, m, partners, full, share, width) for m in range(partners)]
    near = [swap(p[0], m) for m, p in enumerate(packed)]
    far = [lax.ppermute(x, "space", [(0, 1), (1, 0)]) for x in near]

    done = []
    for c in range(CHUNKS):
        queries = near if c == 0 else [swap(p[c], m) for m, p in enumerate(packed)]
        done.append(attend(window, queries, near, far, c, full, share, width, rows_dev))
    begun, shares = [], ()
    for c in range(CHUNKS):
        parts = [swap(x, m) for m, x in enumerate(done[c])]
        common = (parts, out_weight, lax.axis_size("head"), full, share, width)
        if c == 0:
            shares = project(*common, slice(1), [x[0] for x in done[1:]])
            shares += project(*common, slice(1, None))
        else:
            shares = project(*common, slice(1), shares[-1:])
            shares += project(*common, slice(1, None))
        begun.append(begin_sums(shares, "head"))
        if c == 0:
            first, *done[1] = lax.optimization_barrier((shares[0], *done[1]))
    outputs = finish_sums(begun, "head")
    return jnp.concatenate(outputs, axis=0).reshape(frames_dev, rows_dev, width, -1)


def can_exchange(mesh, query, key, value, window, out_weight):
    partners, sides = mesh.shape["tm"], mesh.shape["space"]
    frames, rows, width, feats = query.shape
    heads = feats // HD // mesh.shape["head"]
    rows_dev = rows // sides
    if mesh.shape["head"] != 4:
        return False
    rest = heads % partners
    if partners & (partners - 1) or sides != 2 or frames != partners or rest == 0 or heads < partners:
        return False
    return partners % rest == 0 and rows_dev == CHUNKS * (partners // rest) and width % 16 == 0


def padded_2(x, sides, width):
    for axis, dim in sides:
        size, length = (lax.axis_size(axis), x.shape[dim])
        up = [(i, (i + 1) % size) for i in range(size - 1)]
        down = [(j, i) for i, j in up]
        last = lax.slice_in_dim(x, length - width, length, axis=dim)
        first = lax.slice_in_dim(x, 0, width, axis=dim)
        before = lax.ppermute(last, axis, up)
        after = lax.ppermute(first, axis, down)
        x = jnp.concatenate([before, x, after], axis=dim)
    return x


def frame_mask(widths, query_rows, key_rows, total_rows, width):
    count = widths.shape[0]
    distance = jnp.abs(query_rows[:, None] - key_rows[None, :])
    inside_grid = (key_rows >= 0) & (key_rows < total_rows)
    inside = (
        (widths[:, None, None] >= 0)
        & (distance[None] <= widths[:, None, None])
        & inside_grid[None, None, :]
    )
    span_rows = key_rows.shape[0]
    full = jnp.broadcast_to(
        inside[:, :, None, :, None], (count, query_rows.shape[0], width, span_rows, width)
    )
    return full.reshape(count * query_rows.shape[0] * width, span_rows * width)


def absorb(state, queries, keys, values, mask):
    run_max, run_sum, run_acc = state
    scale = 1.0 / math.sqrt(HD)
    scores = jnp.einsum("qhd,khd->hqk", queries, keys, preferred_element_type=jnp.float32) * scale
    new_max = jnp.maximum(run_max, jnp.max(jnp.where(mask[None], scores, NEG_FILL), axis=-1))
    weights = jnp.where(mask[None], jnp.exp(scores - new_max[..., None]), 0.0)
    factor = jnp.exp(run_max - new_max)
    new_sum = run_sum * factor + jnp.sum(weights, axis=-1)
    new_acc = run_acc * factor[..., None] + jnp.einsum(
        "hqk,khd->hqd", weights.astype(jnp.bfloat16), values, preferred_element_type=jnp.float32
    )
    return (new_max, new_sum, new_acc)


def absorb_frame(state, queries, widths, kv_frame, query_rows, key_rows, total_rows):
    span_rows, width, feats = (kv_frame.shape[1], kv_frame.shape[2], kv_frame.shape[3])
    heads_dev = feats // HD
    keys = kv_frame[0].reshape(span_rows * width, heads_dev, HD)
    values = kv_frame[1].reshape(span_rows * width, heads_dev, HD)
    mask = frame_mask(widths, query_rows, key_rows, total_rows, width)
    return absorb(state, queries, keys, values, mask)


def empty_state(heads_dev, count):
    return (
        jnp.full((heads_dev, count), NEG_FILL, jnp.float32),
        jnp.zeros((heads_dev, count), jnp.float32),
        jnp.zeros((heads_dev, count, HD), jnp.float32),
    )


def gather_plan(query, key, value, window, out_weight):
    frames_dev, rows_dev, width, feats = query.shape
    heads_dev = feats // HD
    qcount = frames_dev * rows_dev * width
    total_rows = rows_dev * lax.axis_size("space")
    first_row = lax.axis_index("space") * rows_dev
    first_frame = lax.axis_index("tm") * frames_dev
    query_rows = first_row + jnp.arange(rows_dev, dtype=jnp.int32)
    stacked = jnp.stack([key, value])
    padded = padded_2(stacked, (("space", 2),), HALO)
    key_rows = first_row - HALO + jnp.arange(rows_dev + 2 * HALO, dtype=jnp.int32)
    my_windows = lax.dynamic_slice_in_dim(window, first_frame, frames_dev, 0)
    queries = query.reshape(qcount, heads_dev, HD)
    piece = lax.all_gather(padded, "tm", axis=1, tiled=True)

    def one_frame(carry, offset):
        kv_frame = lax.dynamic_index_in_dim(piece, offset, 1, False)
        widths = lax.dynamic_index_in_dim(my_windows, offset, 1, False)
        return (
            absorb_frame(carry, queries, widths, kv_frame, query_rows, key_rows, total_rows),
            None,
        )

    result, unused = lax.scan(
        one_frame, empty_state(heads_dev, qcount), jnp.arange(piece.shape[1], dtype=jnp.int32)
    )
    run_max, run_sum, run_acc = result
    attended = (
        (run_acc / run_sum[..., None])
        .transpose(1, 0, 2)
        .reshape(qcount, feats)
        .astype(jnp.bfloat16)
    )
    share_rows = out_weight.shape[1] // lax.axis_size("head")
    mixed = lax.psum_scatter(
        lax.dot_general(
            out_weight, attended, (((0,), (1,)), ((), ())), preferred_element_type=jnp.float32
        ).astype(jnp.bfloat16),
        "head",
        scatter_dimension=0,
        tiled=True,
    ).astype(jnp.float32)
    return mixed.T.reshape(frames_dev, rows_dev, width, share_rows).astype(jnp.bfloat16)


def solution(mesh):
    placed = (
        P("tm", "space", None, "head"),
        P("tm", "space", None, "head"),
        P("tm", "space", None, "head"),
        P(),
        P("head", None),
    )

    def run(*args):
        body = exchange_plan if can_exchange(mesh, *args) else gather_plan
        return jax.shard_map(
            body, mesh=mesh, in_specs=placed, out_specs=P("tm", "space", None, "head"), check_vma=False
        )(*args)

    return run
```

```python
import math

import jax
import jax.numpy as jnp
from jax import lax
from jax.experimental import pallas as pl
from jax.experimental.pallas import tpu as pltpu
from jax.sharding import PartitionSpec as P

HD = 128
HALO = 4
NEG_FILL = -1e30
CHUNKS = 2
VMEM = pltpu.CompilerParams(vmem_limit_bytes=32 * 1024 * 1024)


def pack_kernel(q_ref, k_ref, v_ref, first, *rest, partner, partners, full, share, row):
    sems = rest[-1]
    tokens = q_ref.shape[0]
    part = tokens // CHUNKS
    chip = lax.axis_index("tm") ^ partner
    heads = [chip * full + i for i in range(full)] + [partners * full + chip // share]
    lanes = [pl.ds(pl.multiple_of(h * HD, HD), HD) for h in heads]
    moves = []
    for kind, source in enumerate((k_ref, v_ref)):
        for i, lane in enumerate(lanes):
            place = pl.ds((kind * (full + 1) + i) * tokens, tokens)
            moves.append((source.at[:, lane], first.at[place]))
    for c in range(CHUNKS):
        target, base = (first, 2 * (full + 1) * tokens) if c == 0 else (rest[c - 1], 0)
        for i in range(full):
            moves.append((q_ref.at[pl.ds(c * part, part), lanes[i]], target.at[pl.ds(base + i * part, part)]))
        start = pl.multiple_of(c * part + (chip % share) * row, 16)
        moves.append((q_ref.at[pl.ds(start, row), lanes[full]], target.at[pl.ds(base + full * part, row)]))
    copies = [pltpu.make_async_copy(a, b, sems.at[n]) for n, (a, b) in enumerate(moves)]
    for copy in copies:
        copy.start()
    for copy in copies:
        copy.wait()


def pack(q, k, v, partner, partners, full, share, row):
    direct = partner == partners - 1
    tokens = q.shape[0]
    queries = full * (tokens // CHUNKS) + row
    slabs = 2 * (full + 1) * tokens + queries
    whole = pl.BlockSpec(memory_space=pltpu.VMEM)
    anywhere = pl.BlockSpec(memory_space=pl.ANY)
    shapes = [jax.ShapeDtypeStruct((slabs, HD), q.dtype)]
    shapes += [jax.ShapeDtypeStruct((queries, HD), q.dtype)] * (CHUNKS - 1)

    def kernel(*refs):
        pack_kernel(*refs, partner=partner, partners=partners, full=full, share=share, row=row)

    return pl.pallas_call(
        kernel,
        out_shape=shapes,
        in_specs=[anywhere] * 3,
        out_specs=[whole] * len(shapes),
        scratch_shapes=[pltpu.SemaphoreType.DMA(((full + 1) * (2 + CHUNKS),))],
        compiler_params=pltpu.CompilerParams(vmem_limit_bytes=(60 if direct else 32) * 1024 * 1024),
        name="pack",
    )(q, k, v)


def attend_kernel(
    window_ref, *refs, chunk, partners, full, share, row, rows_dev, total_rows, asked
):
    queries = refs[:partners]
    near = refs[partners : 2 * partners]
    far = refs[2 * partners : 3 * partners]
    outs = refs[3 * partners :]
    slots = full + 1
    tokens = rows_dev * row
    count = 2 * partners * tokens
    t, s = lax.axis_index("tm"), lax.axis_index("space")
    rows_part = rows_dev // CHUNKS
    factor = math.log2(math.e) / math.sqrt(HD)

    at = lax.broadcasted_iota(jnp.int32, (1, count), 1)
    frame = at // (2 * tokens)
    side = (at // tokens) % 2
    key_row = (at % tokens) // row + rows_dev * jnp.where(side == 0, s, 1 - s)
    widths = []
    for m in range(partners):
        wide = jnp.zeros_like(at)
        for m2 in range(partners):
            wide = jnp.where(frame == m2, window_ref[t ^ m, t ^ m2], wide)
        widths.append(wide)

    def bias(unit, m):
        part_row = unit % rows_part if unit < full * rows_part else t % share
        distance = jnp.abs(key_row - (rows_dev * s + rows_part * chunk + part_row))
        return jnp.where(distance <= widths[m], 0.0, NEG_FILL).astype(jnp.float32)

    def block(kind, slot):
        base = (kind * slots + slot) * tokens
        return jnp.concatenate([r[pl.ds(base, tokens)] for m in range(partners) for r in (near[m], far[m])], axis=0)

    def score(tile):
        unit, pair = tile
        q = jnp.concatenate([queries[m][pl.ds(asked + unit * row, row)] for m in pair], axis=0)
        return lax.dot_general(
            q, block(0, unit // rows_part), (((1,), (1,)), ((), ())), preferred_element_type=jnp.float32
        )

    def weigh(tile, scores):
        unit, pair = tile
        scores = jnp.concatenate(
            [scores[i * row : (i + 1) * row] + bias(unit, m) for i, m in enumerate(pair)], axis=0
        )
        top = jnp.max(scores, axis=-1, keepdims=True)
        return jnp.exp2((scores - top) * factor).astype(jnp.bfloat16)

    def gather(tile, weights):
        unit, pair = tile
        held = block(1, unit // rows_part)
        held = jnp.concatenate([held, jnp.ones_like(held)], axis=1)
        summed = jnp.dot(weights, held, preferred_element_type=jnp.float32)
        out = (summed[:, :HD] / summed[:, HD:]).astype(jnp.bfloat16)
        for i, m in enumerate(pair):
            outs[m][pl.ds(unit * row, row)] = out[i * row : (i + 1) * row]

    pairs = [tuple(range(m, m + 2)) for m in range(0, partners, 2)]
    tiles = [(unit, pair) for unit in range(full * rows_part + 1) for pair in pairs]
    scores, last = score(tiles[0]), None
    for i, tile in enumerate(tiles):
        if last is not None:
            gather(*last)
        following = score(tiles[i + 1]) if i + 1 < len(tiles) else None
        last = (tile, weigh(tile, scores))
        scores = following
    gather(*last)


def attend(window, queries, near, far, chunk, full, share, row, rows_dev):
    partners = len(queries)
    rows_out = full * (rows_dev // CHUNKS) * row + row
    count = 2 * partners * rows_dev * row
    whole = pl.BlockSpec(memory_space=pltpu.VMEM)
    scalars = pl.BlockSpec(memory_space=pltpu.SMEM)

    def kernel(*refs):
        attend_kernel(
            *refs,
            chunk=chunk,
            partners=partners,
            full=full,
            share=share,
            row=row,
            rows_dev=rows_dev,
            total_rows=2 * rows_dev,
            asked=queries[0].shape[0] - rows_out,
        )

    work = partners * rows_out * count
    return pl.pallas_call(
        kernel,
        out_shape=[jax.ShapeDtypeStruct((rows_out, HD), jnp.bfloat16)] * partners,
        in_specs=[scalars] + [whole] * (3 * partners),
        out_specs=[whole] * partners,
        compiler_params=VMEM,
        cost_estimate=pl.CostEstimate(
            flops=work * HD * 4, bytes_accessed=count * HD * 4 * (full + 1), transcendentals=work
        ),
        name="attend",
    )(window, *queries, *near, *far)


def shares_sent(place, size):
    wanted = []
    for k in range(1, size):
        right, left = place + size - k, place - size + k
        if 2 * k <= size:
            wanted.append(jnp.where(place < k, right, jnp.maximum(left, 0)))
        else:
            wanted += [jnp.minimum(right, size - 1), jnp.maximum(left, 0)]
    return [*wanted, place]


def project_kernel(*refs, after, partners, full, share, row, size, chosen):
    parts, weight, outs, mixed = refs[:partners], refs[partners], refs[partners + 1 + after : -1], refs[-1]
    part, block = outs[0].shape
    wide = full * HD
    t = lax.axis_index("tm")
    firsts, lasts = [], []
    for m in range(partners):
        for i in range(full):
            mixed[:, m * wide + i * HD : m * wide + (i + 1) * HD] = parts[m][pl.ds(i * part, part)]
        firsts.append((t ^ m) * wide)
        group, offset = divmod(m, share)
        lane = partners * wide + group * HD
        rows = pl.ds(pl.multiple_of((t ^ m) % share * row, 16), row)
        mixed[rows, lane : lane + HD] = parts[m][pl.ds(full * part, row)]
        if offset == 0:
            lasts.append(partners * wide + (t ^ m) // share * HD)
    starts = [(start, wide) for start in firsts] + [(start, HD) for start in lasts]
    for d, out in zip(shares_sent(lax.axis_index("head"), size)[chosen], outs):
        columns = pl.ds(pl.multiple_of(d * block, HD), block)
        rows = [weight[pl.ds(pl.multiple_of(start, HD), n), columns] for start, n in starts]
        product = jnp.dot(mixed[...], jnp.concatenate(rows, axis=0), preferred_element_type=jnp.float32)
        out[...] = product.astype(out.dtype)


def project(parts, weight, size, full, share, row, chosen, after=()):
    partners = len(parts)
    feats, width = weight.shape
    part = (parts[0].shape[0] - row) // full
    count = len(shares_sent(0, size)[chosen])
    whole = pl.BlockSpec(memory_space=pltpu.VMEM)

    def kernel(*refs):
        project_kernel(
            *refs,
            after=len(after),
            partners=partners,
            full=full,
            share=share,
            row=row,
            size=size,
            chosen=chosen,
        )

    return pl.pallas_call(
        kernel,
        out_shape=[jax.ShapeDtypeStruct((part, width // size), jnp.bfloat16)] * count,
        in_specs=[whole] * (partners + 1) + [pl.BlockSpec(memory_space=pl.ANY)] * len(after),
        out_specs=[whole] * count,
        scratch_shapes=[pltpu.VMEM((part, feats), jnp.bfloat16)],
        compiler_params=VMEM,
        cost_estimate=pl.CostEstimate(
            flops=2 * part * feats * width, bytes_accessed=2 * feats * width, transcendentals=0
        ),
        name="project",
    )(*parts, weight, *after)


def begin_sums(shares, axis):
    size = lax.axis_size(axis)
    come = lax.ppermute(shares[0], axis, [(0, 1), (size - 1, size - 2)])
    return shares[1] + come, list(shares[2:])


def finish_sums(begun, axis):
    size = lax.axis_size(axis)
    held = [(sent, sent) for sent, _ in begun]
    for step in range(2, size):
        for c, (_, shares) in enumerate(begun):
            right, left = held[c]
            if step > 2:
                send_right = shares.pop(0)
                send_left = send_right if 2 * step <= size else shares.pop(0)
                right, left = send_right + right, send_left + left
            held[c] = (
                lax.ppermute(right, axis, [(i, i + 1) for i in range(step)]),
                lax.ppermute(left, axis, [(size - 1 - i, size - 2 - i) for i in range(step)]),
            )
    return [own + right + left for (_, (own,)), (right, left) in zip(begun, held)]


def exchange_plan(query, key, value, window, out_weight):
    frames_dev, rows_dev, width, feats = query.shape
    partners = lax.axis_size("tm")
    heads = feats // HD
    full = heads // partners
    share = partners // (heads - full * partners)
    tokens = rows_dev * width
    flat = [a.reshape(tokens, feats) for a in (query, key, value)]

    def swap(x, m):
        return x if m == 0 else lax.ppermute(x, "tm", [(i, i ^ m) for i in range(partners)])

    packed = [pack(*flat, m, partners, full, share, width) for m in range(partners)]
    near = [swap(p[0], m) for m, p in enumerate(packed)]
    far = [lax.ppermute(x, "space", [(0, 1), (1, 0)]) for x in near]

    done = []
    for c in range(CHUNKS):
        queries = near if c == 0 else [swap(p[c], m) for m, p in enumerate(packed)]
        done.append(attend(window, queries, near, far, c, full, share, width, rows_dev))
    begun, shares = [], ()
    for c in range(CHUNKS):
        parts = [swap(x, m) for m, x in enumerate(done[c])]
        common = (parts, out_weight, lax.axis_size("head"), full, share, width)
        if c == 0:
            shares = project(*common, slice(1), [x[0] for x in done[1:]])
            shares += project(*common, slice(1, None))
        else:
            shares = project(*common, slice(1), shares[-1:])
            shares += project(*common, slice(1, None))
        begun.append(begin_sums(shares, "head"))
        if c == 0:
            first, *tied = lax.optimization_barrier((shares[0], *done[1][:-1]))
            done[1] = [*tied, done[1][-1]]
    outputs = finish_sums(begun, "head")
    return jnp.concatenate(outputs, axis=0).reshape(frames_dev, rows_dev, width, -1)


def can_exchange(mesh, query, key, value, window, out_weight):
    partners, sides = mesh.shape["tm"], mesh.shape["space"]
    frames, rows, width, feats = query.shape
    heads = feats // HD // mesh.shape["head"]
    rows_dev = rows // sides
    if mesh.shape["head"] != 4:
        return False
    rest = heads % partners
    if partners & (partners - 1) or sides != 2 or frames != partners or rest == 0 or heads < partners:
        return False
    return partners % rest == 0 and rows_dev == CHUNKS * (partners // rest) and width % 16 == 0


def padded_2(x, sides, width):
    for axis, dim in sides:
        size, length = (lax.axis_size(axis), x.shape[dim])
        up = [(i, (i + 1) % size) for i in range(size - 1)]
        down = [(j, i) for i, j in up]
        last = lax.slice_in_dim(x, length - width, length, axis=dim)
        first = lax.slice_in_dim(x, 0, width, axis=dim)
        before = lax.ppermute(last, axis, up)
        after = lax.ppermute(first, axis, down)
        x = jnp.concatenate([before, x, after], axis=dim)
    return x


def frame_mask(widths, query_rows, key_rows, total_rows, width):
    count = widths.shape[0]
    distance = jnp.abs(query_rows[:, None] - key_rows[None, :])
    inside_grid = (key_rows >= 0) & (key_rows < total_rows)
    inside = (
        (widths[:, None, None] >= 0)
        & (distance[None] <= widths[:, None, None])
        & inside_grid[None, None, :]
    )
    span_rows = key_rows.shape[0]
    full = jnp.broadcast_to(
        inside[:, :, None, :, None], (count, query_rows.shape[0], width, span_rows, width)
    )
    return full.reshape(count * query_rows.shape[0] * width, span_rows * width)


def absorb(state, queries, keys, values, mask):
    run_max, run_sum, run_acc = state
    scale = 1.0 / math.sqrt(HD)
    scores = jnp.einsum("qhd,khd->hqk", queries, keys, preferred_element_type=jnp.float32) * scale
    new_max = jnp.maximum(run_max, jnp.max(jnp.where(mask[None], scores, NEG_FILL), axis=-1))
    weights = jnp.where(mask[None], jnp.exp(scores - new_max[..., None]), 0.0)
    factor = jnp.exp(run_max - new_max)
    new_sum = run_sum * factor + jnp.sum(weights, axis=-1)
    new_acc = run_acc * factor[..., None] + jnp.einsum(
        "hqk,khd->hqd", weights.astype(jnp.bfloat16), values, preferred_element_type=jnp.float32
    )
    return (new_max, new_sum, new_acc)


def absorb_frame(state, queries, widths, kv_frame, query_rows, key_rows, total_rows):
    span_rows, width, feats = (kv_frame.shape[1], kv_frame.shape[2], kv_frame.shape[3])
    heads_dev = feats // HD
    keys = kv_frame[0].reshape(span_rows * width, heads_dev, HD)
    values = kv_frame[1].reshape(span_rows * width, heads_dev, HD)
    mask = frame_mask(widths, query_rows, key_rows, total_rows, width)
    return absorb(state, queries, keys, values, mask)


def empty_state(heads_dev, count):
    return (
        jnp.full((heads_dev, count), NEG_FILL, jnp.float32),
        jnp.zeros((heads_dev, count), jnp.float32),
        jnp.zeros((heads_dev, count, HD), jnp.float32),
    )


def gather_plan(query, key, value, window, out_weight):
    frames_dev, rows_dev, width, feats = query.shape
    heads_dev = feats // HD
    qcount = frames_dev * rows_dev * width
    total_rows = rows_dev * lax.axis_size("space")
    first_row = lax.axis_index("space") * rows_dev
    first_frame = lax.axis_index("tm") * frames_dev
    query_rows = first_row + jnp.arange(rows_dev, dtype=jnp.int32)
    stacked = jnp.stack([key, value])
    padded = padded_2(stacked, (("space", 2),), HALO)
    key_rows = first_row - HALO + jnp.arange(rows_dev + 2 * HALO, dtype=jnp.int32)
    my_windows = lax.dynamic_slice_in_dim(window, first_frame, frames_dev, 0)
    queries = query.reshape(qcount, heads_dev, HD)
    piece = lax.all_gather(padded, "tm", axis=1, tiled=True)

    def one_frame(carry, offset):
        kv_frame = lax.dynamic_index_in_dim(piece, offset, 1, False)
        widths = lax.dynamic_index_in_dim(my_windows, offset, 1, False)
        return (
            absorb_frame(carry, queries, widths, kv_frame, query_rows, key_rows, total_rows),
            None,
        )

    result, unused = lax.scan(
        one_frame, empty_state(heads_dev, qcount), jnp.arange(piece.shape[1], dtype=jnp.int32)
    )
    run_max, run_sum, run_acc = result
    attended = (
        (run_acc / run_sum[..., None])
        .transpose(1, 0, 2)
        .reshape(qcount, feats)
        .astype(jnp.bfloat16)
    )
    share_rows = out_weight.shape[1] // lax.axis_size("head")
    mixed = lax.psum_scatter(
        lax.dot_general(
            out_weight, attended, (((0,), (1,)), ((), ())), preferred_element_type=jnp.float32
        ).astype(jnp.bfloat16),
        "head",
        scatter_dimension=0,
        tiled=True,
    ).astype(jnp.float32)
    return mixed.T.reshape(frames_dev, rows_dev, width, share_rows).astype(jnp.bfloat16)


def solution(mesh):
    placed = (
        P("tm", "space", None, "head"),
        P("tm", "space", None, "head"),
        P("tm", "space", None, "head"),
        P(),
        P("head", None),
    )

    def run(*args):
        body = exchange_plan if can_exchange(mesh, *args) else gather_plan
        return jax.shard_map(
            body, mesh=mesh, in_specs=placed, out_specs=P("tm", "space", None, "head"), check_vma=False
        )(*args)

    return run
```

```python
import math

import jax
import jax.numpy as jnp
from jax import lax
from jax.experimental import pallas as pl
from jax.experimental.pallas import tpu as pltpu
from jax.sharding import PartitionSpec as P

HD = 128
HALO = 4
NEG_FILL = -1e30
CHUNKS = 2
VMEM = pltpu.CompilerParams(vmem_limit_bytes=32 * 1024 * 1024)


def pack_kernel(q_ref, k_ref, v_ref, first, *rest, partner, partners, full, share, row):
    sems = rest[-1]
    tokens = q_ref.shape[0]
    part = tokens // CHUNKS
    chip = lax.axis_index("tm") ^ partner
    heads = [chip * full + i for i in range(full)] + [partners * full + chip // share]
    lanes = [pl.ds(pl.multiple_of(h * HD, HD), HD) for h in heads]
    moves = []
    for kind, source in enumerate((k_ref, v_ref)):
        for i, lane in enumerate(lanes):
            place = pl.ds((kind * (full + 1) + i) * tokens, tokens)
            moves.append((source.at[:, lane], first.at[place]))
    for c in range(CHUNKS):
        target, base = (first, 2 * (full + 1) * tokens) if c == 0 else (rest[c - 1], 0)
        for i in range(full):
            moves.append((q_ref.at[pl.ds(c * part, part), lanes[i]], target.at[pl.ds(base + i * part, part)]))
        start = pl.multiple_of(c * part + (chip % share) * row, 16)
        moves.append((q_ref.at[pl.ds(start, row), lanes[full]], target.at[pl.ds(base + full * part, row)]))
    copies = [pltpu.make_async_copy(a, b, sems.at[n]) for n, (a, b) in enumerate(moves)]
    for copy in copies:
        copy.start()
    for copy in copies:
        copy.wait()


def pack(q, k, v, partner, partners, full, share, row):
    direct = partner == partners - 1
    tokens = q.shape[0]
    queries = full * (tokens // CHUNKS) + row
    slabs = 2 * (full + 1) * tokens + queries
    whole = pl.BlockSpec(memory_space=pltpu.VMEM)
    anywhere = pl.BlockSpec(memory_space=pl.ANY)
    shapes = [jax.ShapeDtypeStruct((slabs, HD), q.dtype)]
    shapes += [jax.ShapeDtypeStruct((queries, HD), q.dtype)] * (CHUNKS - 1)

    def kernel(*refs):
        pack_kernel(*refs, partner=partner, partners=partners, full=full, share=share, row=row)

    return pl.pallas_call(
        kernel,
        out_shape=shapes,
        in_specs=[anywhere] * 3,
        out_specs=[whole] * len(shapes),
        scratch_shapes=[pltpu.SemaphoreType.DMA(((full + 1) * (2 + CHUNKS),))],
        compiler_params=pltpu.CompilerParams(vmem_limit_bytes=(60 if direct else 32) * 1024 * 1024),
        name="pack",
    )(q, k, v)


def attend_kernel(
    window_ref, *refs, chunk, partners, full, share, row, rows_dev, total_rows, asked
):
    queries = refs[:partners]
    near = refs[partners : 2 * partners]
    far = refs[2 * partners : 3 * partners]
    outs = refs[3 * partners :]
    slots = full + 1
    tokens = rows_dev * row
    count = 2 * partners * tokens
    t, s = lax.axis_index("tm"), lax.axis_index("space")
    rows_part = rows_dev // CHUNKS
    factor = math.log2(math.e) / math.sqrt(HD)

    at = lax.broadcasted_iota(jnp.int32, (1, count), 1)
    frame = at // (2 * tokens)
    side = (at // tokens) % 2
    key_row = (at % tokens) // row + rows_dev * jnp.where(side == 0, s, 1 - s)
    widths = []
    for m in range(partners):
        wide = jnp.zeros_like(at)
        for m2 in range(partners):
            wide = jnp.where(frame == m2, window_ref[t ^ m, t ^ m2], wide)
        widths.append(wide)

    def bias(unit, m):
        part_row = unit % rows_part if unit < full * rows_part else t % share
        distance = jnp.abs(key_row - (rows_dev * s + rows_part * chunk + part_row))
        return jnp.where(distance <= widths[m], 0.0, NEG_FILL).astype(jnp.float32)

    def block(kind, slot):
        base = (kind * slots + slot) * tokens
        return jnp.concatenate([r[pl.ds(base, tokens)] for m in range(partners) for r in (near[m], far[m])], axis=0)

    def score(tile):
        unit, pair = tile
        q = jnp.concatenate([queries[m][pl.ds(asked + unit * row, row)] for m in pair], axis=0)
        return lax.dot_general(
            q, block(0, unit // rows_part), (((1,), (1,)), ((), ())), preferred_element_type=jnp.float32
        )

    def weigh(tile, scores):
        unit, pair = tile
        scores = jnp.concatenate(
            [scores[i * row : (i + 1) * row] + bias(unit, m) for i, m in enumerate(pair)], axis=0
        )
        top = jnp.max(scores, axis=-1, keepdims=True)
        return jnp.exp2((scores - top) * factor).astype(jnp.bfloat16)

    def gather(tile, weights):
        unit, pair = tile
        held = block(1, unit // rows_part)
        held = jnp.concatenate([held, jnp.ones_like(held)], axis=1)
        summed = jnp.dot(weights, held, preferred_element_type=jnp.float32)
        out = (summed[:, :HD] / summed[:, HD:]).astype(jnp.bfloat16)
        for i, m in enumerate(pair):
            outs[m][pl.ds(unit * row, row)] = out[i * row : (i + 1) * row]

    pairs = [tuple(range(m, m + 2)) for m in range(0, partners, 2)]
    tiles = [(unit, pair) for unit in range(full * rows_part + 1) for pair in pairs]
    scores, last = score(tiles[0]), None
    for i, tile in enumerate(tiles):
        now = (tile, weigh(tile, scores))
        if last is not None:
            gather(*last)
        scores = score(tiles[i + 1]) if i + 1 < len(tiles) else None
        last = now
    gather(*last)


def attend(window, queries, near, far, chunk, full, share, row, rows_dev):
    partners = len(queries)
    rows_out = full * (rows_dev // CHUNKS) * row + row
    count = 2 * partners * rows_dev * row
    whole = pl.BlockSpec(memory_space=pltpu.VMEM)
    scalars = pl.BlockSpec(memory_space=pltpu.SMEM)

    def kernel(*refs):
        attend_kernel(
            *refs,
            chunk=chunk,
            partners=partners,
            full=full,
            share=share,
            row=row,
            rows_dev=rows_dev,
            total_rows=2 * rows_dev,
            asked=queries[0].shape[0] - rows_out,
        )

    work = partners * rows_out * count
    return pl.pallas_call(
        kernel,
        out_shape=[jax.ShapeDtypeStruct((rows_out, HD), jnp.bfloat16)] * partners,
        in_specs=[scalars] + [whole] * (3 * partners),
        out_specs=[whole] * partners,
        compiler_params=VMEM,
        cost_estimate=pl.CostEstimate(
            flops=work * HD * 4, bytes_accessed=count * HD * 4 * (full + 1), transcendentals=work
        ),
        name="attend",
    )(window, *queries, *near, *far)


def shares_sent(place, size):
    wanted = []
    for k in range(1, size):
        right, left = place + size - k, place - size + k
        if 2 * k <= size:
            wanted.append(jnp.where(place < k, right, jnp.maximum(left, 0)))
        else:
            wanted += [jnp.minimum(right, size - 1), jnp.maximum(left, 0)]
    return [*wanted, place]


def project_kernel(*refs, after, partners, full, share, row, size, chosen):
    parts, weight, outs, mixed = refs[:partners], refs[partners], refs[partners + 1 + after : -1], refs[-1]
    part, block = outs[0].shape
    wide = full * HD
    t = lax.axis_index("tm")
    firsts, lasts = [], []
    for m in range(partners):
        for i in range(full):
            mixed[:, m * wide + i * HD : m * wide + (i + 1) * HD] = parts[m][pl.ds(i * part, part)]
        firsts.append((t ^ m) * wide)
        group, offset = divmod(m, share)
        lane = partners * wide + group * HD
        rows = pl.ds(pl.multiple_of((t ^ m) % share * row, 16), row)
        mixed[rows, lane : lane + HD] = parts[m][pl.ds(full * part, row)]
        if offset == 0:
            lasts.append(partners * wide + (t ^ m) // share * HD)
    starts = [(start, wide) for start in firsts] + [(start, HD) for start in lasts]
    for d, out in zip(shares_sent(lax.axis_index("head"), size)[chosen], outs):
        columns = pl.ds(pl.multiple_of(d * block, HD), block)
        rows = [weight[pl.ds(pl.multiple_of(start, HD), n), columns] for start, n in starts]
        product = jnp.dot(mixed[...], jnp.concatenate(rows, axis=0), preferred_element_type=jnp.float32)
        out[...] = product.astype(out.dtype)


def project(parts, weight, size, full, share, row, chosen, after=()):
    partners = len(parts)
    feats, width = weight.shape
    part = (parts[0].shape[0] - row) // full
    count = len(shares_sent(0, size)[chosen])
    whole = pl.BlockSpec(memory_space=pltpu.VMEM)

    def kernel(*refs):
        project_kernel(
            *refs,
            after=len(after),
            partners=partners,
            full=full,
            share=share,
            row=row,
            size=size,
            chosen=chosen,
        )

    return pl.pallas_call(
        kernel,
        out_shape=[jax.ShapeDtypeStruct((part, width // size), jnp.bfloat16)] * count,
        in_specs=[whole] * (partners + 1) + [pl.BlockSpec(memory_space=pl.ANY)] * len(after),
        out_specs=[whole] * count,
        scratch_shapes=[pltpu.VMEM((part, feats), jnp.bfloat16)],
        compiler_params=VMEM,
        cost_estimate=pl.CostEstimate(
            flops=2 * part * feats * width, bytes_accessed=2 * feats * width, transcendentals=0
        ),
        name="project",
    )(*parts, weight, *after)


def begin_sums(shares, axis):
    size = lax.axis_size(axis)
    come = lax.ppermute(shares[0], axis, [(0, 1), (size - 1, size - 2)])
    return shares[1] + come, list(shares[2:])


def finish_sums(begun, axis):
    size = lax.axis_size(axis)
    held = [(sent, sent) for sent, _ in begun]
    for step in range(2, size):
        for c, (_, shares) in enumerate(begun):
            right, left = held[c]
            if step > 2:
                send_right = shares.pop(0)
                send_left = send_right if 2 * step <= size else shares.pop(0)
                right, left = send_right + right, send_left + left
            held[c] = (
                lax.ppermute(right, axis, [(i, i + 1) for i in range(step)]),
                lax.ppermute(left, axis, [(size - 1 - i, size - 2 - i) for i in range(step)]),
            )
    return [own + right + left for (_, (own,)), (right, left) in zip(begun, held)]


def exchange_plan(query, key, value, window, out_weight):
    frames_dev, rows_dev, width, feats = query.shape
    partners = lax.axis_size("tm")
    heads = feats // HD
    full = heads // partners
    share = partners // (heads - full * partners)
    tokens = rows_dev * width
    flat = [a.reshape(tokens, feats) for a in (query, key, value)]

    def swap(x, m):
        return x if m == 0 else lax.ppermute(x, "tm", [(i, i ^ m) for i in range(partners)])

    packed = [pack(*flat, m, partners, full, share, width) for m in range(partners)]
    near = [swap(p[0], m) for m, p in enumerate(packed)]
    far = [lax.ppermute(x, "space", [(0, 1), (1, 0)]) for x in near]

    done = []
    for c in range(CHUNKS):
        queries = near if c == 0 else [swap(p[c], m) for m, p in enumerate(packed)]
        done.append(attend(window, queries, near, far, c, full, share, width, rows_dev))
    begun, shares = [], ()
    for c in range(CHUNKS):
        parts = [swap(x, m) for m, x in enumerate(done[c])]
        common = (parts, out_weight, lax.axis_size("head"), full, share, width)
        if c == 0:
            shares = project(*common, slice(1), [x[0] for x in done[1:]])
            shares += project(*common, slice(1, None))
        else:
            shares = project(*common, slice(1), shares[-1:])
            shares += project(*common, slice(1, None))
        begun.append(begin_sums(shares, "head"))
        if c == 0:
            first, *done[1] = lax.optimization_barrier((shares[0], *done[1]))
    outputs = finish_sums(begun, "head")
    return jnp.concatenate(outputs, axis=0).reshape(frames_dev, rows_dev, width, -1)


def can_exchange(mesh, query, key, value, window, out_weight):
    partners, sides = mesh.shape["tm"], mesh.shape["space"]
    frames, rows, width, feats = query.shape
    heads = feats // HD // mesh.shape["head"]
    rows_dev = rows // sides
    if mesh.shape["head"] != 4:
        return False
    rest = heads % partners
    if partners & (partners - 1) or sides != 2 or frames != partners or rest == 0 or heads < partners:
        return False
    return partners % rest == 0 and rows_dev == CHUNKS * (partners // rest) and width % 16 == 0


def padded_2(x, sides, width):
    for axis, dim in sides:
        size, length = (lax.axis_size(axis), x.shape[dim])
        up = [(i, (i + 1) % size) for i in range(size - 1)]
        down = [(j, i) for i, j in up]
        last = lax.slice_in_dim(x, length - width, length, axis=dim)
        first = lax.slice_in_dim(x, 0, width, axis=dim)
        before = lax.ppermute(last, axis, up)
        after = lax.ppermute(first, axis, down)
        x = jnp.concatenate([before, x, after], axis=dim)
    return x


def frame_mask(widths, query_rows, key_rows, total_rows, width):
    count = widths.shape[0]
    distance = jnp.abs(query_rows[:, None] - key_rows[None, :])
    inside_grid = (key_rows >= 0) & (key_rows < total_rows)
    inside = (
        (widths[:, None, None] >= 0)
        & (distance[None] <= widths[:, None, None])
        & inside_grid[None, None, :]
    )
    span_rows = key_rows.shape[0]
    full = jnp.broadcast_to(
        inside[:, :, None, :, None], (count, query_rows.shape[0], width, span_rows, width)
    )
    return full.reshape(count * query_rows.shape[0] * width, span_rows * width)


def absorb(state, queries, keys, values, mask):
    run_max, run_sum, run_acc = state
    scale = 1.0 / math.sqrt(HD)
    scores = jnp.einsum("qhd,khd->hqk", queries, keys, preferred_element_type=jnp.float32) * scale
    new_max = jnp.maximum(run_max, jnp.max(jnp.where(mask[None], scores, NEG_FILL), axis=-1))
    weights = jnp.where(mask[None], jnp.exp(scores - new_max[..., None]), 0.0)
    factor = jnp.exp(run_max - new_max)
    new_sum = run_sum * factor + jnp.sum(weights, axis=-1)
    new_acc = run_acc * factor[..., None] + jnp.einsum(
        "hqk,khd->hqd", weights.astype(jnp.bfloat16), values, preferred_element_type=jnp.float32
    )
    return (new_max, new_sum, new_acc)


def absorb_frame(state, queries, widths, kv_frame, query_rows, key_rows, total_rows):
    span_rows, width, feats = (kv_frame.shape[1], kv_frame.shape[2], kv_frame.shape[3])
    heads_dev = feats // HD
    keys = kv_frame[0].reshape(span_rows * width, heads_dev, HD)
    values = kv_frame[1].reshape(span_rows * width, heads_dev, HD)
    mask = frame_mask(widths, query_rows, key_rows, total_rows, width)
    return absorb(state, queries, keys, values, mask)


def empty_state(heads_dev, count):
    return (
        jnp.full((heads_dev, count), NEG_FILL, jnp.float32),
        jnp.zeros((heads_dev, count), jnp.float32),
        jnp.zeros((heads_dev, count, HD), jnp.float32),
    )


def gather_plan(query, key, value, window, out_weight):
    frames_dev, rows_dev, width, feats = query.shape
    heads_dev = feats // HD
    qcount = frames_dev * rows_dev * width
    total_rows = rows_dev * lax.axis_size("space")
    first_row = lax.axis_index("space") * rows_dev
    first_frame = lax.axis_index("tm") * frames_dev
    query_rows = first_row + jnp.arange(rows_dev, dtype=jnp.int32)
    stacked = jnp.stack([key, value])
    padded = padded_2(stacked, (("space", 2),), HALO)
    key_rows = first_row - HALO + jnp.arange(rows_dev + 2 * HALO, dtype=jnp.int32)
    my_windows = lax.dynamic_slice_in_dim(window, first_frame, frames_dev, 0)
    queries = query.reshape(qcount, heads_dev, HD)
    piece = lax.all_gather(padded, "tm", axis=1, tiled=True)

    def one_frame(carry, offset):
        kv_frame = lax.dynamic_index_in_dim(piece, offset, 1, False)
        widths = lax.dynamic_index_in_dim(my_windows, offset, 1, False)
        return (
            absorb_frame(carry, queries, widths, kv_frame, query_rows, key_rows, total_rows),
            None,
        )

    result, unused = lax.scan(
        one_frame, empty_state(heads_dev, qcount), jnp.arange(piece.shape[1], dtype=jnp.int32)
    )
    run_max, run_sum, run_acc = result
    attended = (
        (run_acc / run_sum[..., None])
        .transpose(1, 0, 2)
        .reshape(qcount, feats)
        .astype(jnp.bfloat16)
    )
    share_rows = out_weight.shape[1] // lax.axis_size("head")
    mixed = lax.psum_scatter(
        lax.dot_general(
            out_weight, attended, (((0,), (1,)), ((), ())), preferred_element_type=jnp.float32
        ).astype(jnp.bfloat16),
        "head",
        scatter_dimension=0,
        tiled=True,
    ).astype(jnp.float32)
    return mixed.T.reshape(frames_dev, rows_dev, width, share_rows).astype(jnp.bfloat16)


def solution(mesh):
    placed = (
        P("tm", "space", None, "head"),
        P("tm", "space", None, "head"),
        P("tm", "space", None, "head"),
        P(),
        P("head", None),
    )

    def run(*args):
        body = exchange_plan if can_exchange(mesh, *args) else gather_plan
        return jax.shard_map(
            body, mesh=mesh, in_specs=placed, out_specs=P("tm", "space", None, "head"), check_vma=False
        )(*args)

    return run
```
